128 devices in a mesh: replica: 8 (over y, core), tensor: 16 (over z, x).
Axes of the slice: x: 4, y: 4, z: 4, core: 2. Of those that a mesh axis runs over, the one named last changes fastest.
Arguments:
- gradient: bfloat16 [8, 6144, 6144], P('replica', None, 'tensor'), may hold values from -40 to 40
- feedback: bfloat16 [8, 6144, 6144], P('replica', None, 'tensor'), may hold values from -6 to 6
- momentum: bfloat16 [6144, 6144], P('replica', 'tensor'), may hold values from -4 to 4
- right_init: float32 [6144, 8], P('tensor'), may hold values from -6 to 6
Outputs:
- feedback_out: bfloat16 [8, 6144, 6144], P('replica', None, 'tensor')
- momentum_out: bfloat16 [6144, 6144], P('replica', 'tensor')
- right_factor: float32 [6144, 8], P('tensor')
The draws below stay inside these ranges and needn't reach their ends.
All inputs are finite; a program needn't handle non-finite values.
Results may differ from the reference program's by a relative error of at most 0.012.
Values sent between devices are 32-bit elements; how exact they have to be, the bound alone decides.
No kernel may reach another device: no remote copies, remote signals or barrier semaphores. Data moves between devices by JAX's collectives and lax.ppermute only.
A program may use at most 64 MiB of HBM per device.

```python
import jax
import jax.numpy as jnp
from jax import lax

D = 6144
DQ = 6144
R = 8
REPLICAS = 8


def draw_gradient(key, part):
    key = jax.random.fold_in(key, 11)
    subkeys = jax.random.split(key, 3)
    left_vecs = jnp.clip(jax.random.normal(subkeys[0], (REPLICAS, D, 4), jnp.float32), -3.0, 3.0)
    right_vecs = jnp.clip(jax.random.normal(subkeys[1], (REPLICAS, DQ, 4), jnp.float32), -3.0, 3.0)
    noise_part = jnp.clip(0.5 * jax.random.normal(subkeys[2], (REPLICAS, D, DQ), jnp.float32), -2.0, 2.0)
    scales = (1.5, 1.0, 0.75, 0.5)
    summed = noise_part
    for index in range(4):
        summed = summed + scales[index] * left_vecs[:, :, index, None] * right_vecs[:, None, :, index]
    return summed.astype(jnp.bfloat16)


def steps_of(stream_key, dims, shards, smallest, largest):
    def one(position, shards_of):
        steps = jax.random.uniform(jax.random.fold_in(jax.random.fold_in(stream_key, 6), position), (shards_of,), jnp.float32, smallest / len(shards), largest / len(shards))
        return jnp.repeat(jnp.exp(steps), dims[position] // shards_of).reshape((-1,) + (1,) * (len(dims) - position - 1))

    level = one(*shards[0])
    for cut in shards[1:]:
        level = level * one(*cut)
    return level


def noise(own_key, extent, deviation, bound, cuts=(), kind=jnp.bfloat16):
    values = jax.random.normal(own_key, extent, jnp.float32) * deviation
    if len(cuts) > 0:
        values = steps_of(own_key, extent, cuts, -0.22, 0.18) * values
    return jnp.clip(values, min=-bound, max=bound).astype(kind)


def setup_inputs(seed: int = 0) -> dict:
    splits = jax.random.split(jax.random.key(seed), 5)
    gradient = draw_gradient(jax.random.fold_in(splits[4], 71), 0)
    feedback = noise(splits[1], (REPLICAS, D, DQ), 1.0, 6.0, ((0, 8), (2, 16)))
    momentum = noise(splits[2], (D, DQ), 0.5, 4.0, ((0, 8), (1, 16)))
    right_init = noise(splits[3], (DQ, R), 1.0, 6.0, ((0, 16),), jnp.float32)
    return dict(gradient=gradient, feedback=feedback, momentum=momentum, right_init=right_init)


def reference(gradient, feedback, momentum, right_init):
    merged = (gradient.astype(jnp.float32) + feedback.astype(jnp.float32)).astype(jnp.bfloat16)
    right_bf = right_init.astype(jnp.bfloat16)
    left_factor = jnp.zeros((D, R), jnp.float32)
    for replica_index in range(REPLICAS):
        left_factor = left_factor + jnp.dot(merged[replica_index].astype(jnp.float32), right_bf.astype(jnp.float32), preferred_element_type=jnp.float32)
    gram_matrix = jnp.dot(left_factor.T, left_factor, precision=lax.Precision.HIGHEST)
    factor_low = jnp.linalg.cholesky(gram_matrix)
    basis_full = lax.linalg.triangular_solve(factor_low, left_factor, left_side=False, lower=True, transpose_a=True)
    basis_bf = basis_full.astype(jnp.bfloat16)
    right_factor = jnp.zeros((DQ, R), jnp.float32)
    for replica_index in range(REPLICAS):
        right_factor = right_factor + jnp.dot(merged[replica_index].T.astype(jnp.float32), basis_bf.astype(jnp.float32), preferred_element_type=jnp.float32)
    right_factor = right_factor / REPLICAS
    approx = jnp.dot(basis_full, right_factor.T, precision=lax.Precision.HIGHEST)
    feedback_out = (merged.astype(jnp.float32) - approx[None]).astype(jnp.bfloat16)
    momentum_out = (0.9 * momentum.astype(jnp.float32) + approx).astype(jnp.bfloat16)
    return (feedback_out, momentum_out, right_factor)
```

```python
import jax
import jax.numpy as jnp
from jax import lax
from jax.experimental import pallas as pl
from jax.experimental.pallas import tpu as pltpu
from jax.sharding import PartitionSpec as P

F32, BF16 = jnp.float32, jnp.bfloat16
ROWS, COLS, RANK = 6144, 384, 8
HALF = ROWS // 2
BLOCK = 512
STEPS = ROWS // BLOCK
MIB = 1 << 20


def core_index():
    return lax.rem(lax.axis_index("replica"), 2)


def split(x):
    high = x.astype(BF16)
    return high, (x - high.astype(F32)).astype(BF16)


def merge_kernel(g_ref, f_ref, q_ref, merged_ref, keep_ref, send_ref):
    step = pl.program_id(0)
    merged = (g_ref[0].astype(F32) + f_ref[0].astype(F32)).astype(BF16)
    merged_ref[pl.ds(pl.multiple_of(step * BLOCK, BLOCK), BLOCK), :] = merged
    term = lax.dot_general(
        q_ref[...].astype(BF16), merged, (((1,), (1,)), ((), ())), preferred_element_type=F32
    )
    per_half = STEPS // 2
    where = pl.ds(pl.multiple_of(lax.rem(step, per_half) * BLOCK, BLOCK), BLOCK)
    mine = (step // per_half) == core_index()

    @pl.when(mine)
    def _():
        keep_ref[:, where] = term

    @pl.when(jnp.logical_not(mine))
    def _():
        send_ref[:, where] = term


def whole():
    return pl.BlockSpec(memory_space=pltpu.VMEM)


def merge(gradient, feedback, right_t):
    block = pl.BlockSpec((1, BLOCK, COLS), lambda i: (0, i, 0))
    return pl.pallas_call(
        merge_kernel,
        grid=(STEPS,),
        in_specs=[block, block, whole()],
        out_specs=[whole(), whole(), whole()],
        out_shape=[
            pltpu.VMEM((ROWS, COLS), BF16),
            pltpu.VMEM((RANK, HALF), F32),
            pltpu.VMEM((RANK, HALF), F32),
        ],
        compiler_params=pltpu.CompilerParams(vmem_limit_bytes=16 * MIB),
        cost_estimate=pl.CostEstimate(flops=2 * ROWS * COLS * RANK, bytes_accessed=4 * ROWS * COLS, transcendentals=0),
        name="merge",
    )(gradient, feedback, right_t)


def right_kernel(merged_ref, own_ref, other_ref, out_ref):
    core = core_index()
    total = jnp.zeros((2 * RANK, COLS), F32)
    for ref, half in ((own_ref, core), (other_ref, 1 - core)):
        rows = pl.ds(pl.multiple_of(half * HALF, HALF), HALF)
        pair = jnp.concatenate(split(ref[...]), axis=0)
        total += jnp.dot(pair, merged_ref[rows, :], preferred_element_type=F32)
    out_ref[...] = total[:RANK] + total[RANK:]


def right_term(merged, own, other):
    return pl.pallas_call(
        right_kernel,
        in_specs=[whole(), whole(), whole()],
        out_specs=whole(),
        out_shape=pltpu.VMEM((RANK, COLS), F32),
        compiler_params=pltpu.CompilerParams(vmem_limit_bytes=16 * MIB),
        cost_estimate=pl.CostEstimate(flops=4 * ROWS * COLS * RANK, bytes_accessed=2 * ROWS * COLS, transcendentals=0),
        name="right_term",
    )(merged, own, other)


def basis_kernel(own_ref, other_ref, inverse_ref, basis_ref):
    own, other = own_ref[...], other_ref[...]
    gram = jnp.zeros((RANK, RANK), F32)
    for part in (own, other):
        gram += lax.dot_general(
            part, part, (((1,), (1,)), ((), ())), precision=lax.Precision.HIGHEST, preferred_element_type=F32
        )
    row = lax.broadcasted_iota(jnp.int32, (RANK, RANK), 0)
    column = lax.broadcasted_iota(jnp.int32, (RANK, RANK), 1)
    eye = jnp.where(row == column, 1.0, 0.0)
    inverse = eye
    for k in range(RANK):
        factor = jnp.where(row[:, :1] > k, gram[:, k : k + 1] / gram[k : k + 1, k : k + 1], 0.0)
        inverse -= factor * inverse[k : k + 1, :]
        gram -= factor * gram[k : k + 1, :]
    pivots = jnp.sum(gram * eye, axis=1, keepdims=True)
    inverse = inverse / jnp.sqrt(pivots)
    inverse_ref[...] = inverse
    core = core_index()
    for part, half in ((own, core), (other, 1 - core)):
        basis = jnp.zeros((RANK, HALF), F32)
        for k in range(RANK):
            basis += inverse[:, k : k + 1] * part[k : k + 1, :]
        high, low = split(basis)
        packed = jnp.concatenate([high, high, low, low], axis=0)
        basis_ref[pl.ds(pl.multiple_of(half * HALF, HALF), HALF), :] = packed.T


def make_basis(own, other):
    return pl.pallas_call(
        basis_kernel,
        in_specs=[whole(), whole()],
        out_specs=[whole(), whole()],
        out_shape=[pltpu.VMEM((RANK, RANK), F32), pltpu.VMEM((ROWS, 4 * RANK), BF16)],
        compiler_params=pltpu.CompilerParams(vmem_limit_bytes=16 * MIB),
        cost_estimate=pl.CostEstimate(flops=4 * ROWS * RANK * RANK, bytes_accessed=4 * MIB, transcendentals=0),
        name="basis",
    )(own, other)


def final_kernel(replicas, merged_ref, basis_ref, inverse_ref, sum_ref, mom_ref, fb_ref, mom_out_ref, right_ref, pack_ref):
    step = pl.program_id(0)

    @pl.when(step == 0)
    def _():
        right = jnp.zeros((RANK, COLS), F32)
        for k in range(RANK):
            right += inverse_ref[:, k : k + 1] * sum_ref[k : k + 1, :]
        right = right * (1.0 / replicas)
        right_ref[...] = right
        high, low = split(right)
        pack_ref[...] = jnp.concatenate([high, low, high, low], axis=0)

    pack = pack_ref[...]
    rows = pl.ds(pl.multiple_of(step * BLOCK, BLOCK), BLOCK)
    approx = jnp.dot(basis_ref[rows, :], pack, preferred_element_type=F32)
    fb_ref[0] = (merged_ref[rows, :].astype(F32) - approx).astype(BF16)
    count = mom_ref.shape[0]
    start = lax.axis_index("replica") * (count * STEPS) + step * count
    mom_rows = pl.ds(pl.multiple_of(start, count), count)
    mom_approx = jnp.dot(basis_ref[mom_rows, :], pack, preferred_element_type=F32)
    mom_out_ref[...] = (0.9 * mom_ref[...].astype(F32) + mom_approx).astype(BF16)


def finish(replicas, merged, basis, inverse, right_sum, momentum):
    mom_rows = momentum.shape[0]
    mom_block = pl.BlockSpec((mom_rows // STEPS, COLS), lambda i: (i, 0))

    def body(*refs):
        final_kernel(replicas, *refs)

    return pl.pallas_call(
        body,
        grid=(STEPS,),
        in_specs=[whole(), whole(), whole(), whole(), mom_block],
        out_specs=[pl.BlockSpec((1, BLOCK, COLS), lambda i: (0, i, 0)), mom_block, whole()],
        out_shape=[
            jax.ShapeDtypeStruct((1, ROWS, COLS), BF16),
            jax.ShapeDtypeStruct((mom_rows, COLS), BF16),
            jax.ShapeDtypeStruct((RANK, COLS), F32),
        ],
        scratch_shapes=[pltpu.VMEM((4 * RANK, COLS), BF16)],
        compiler_params=pltpu.CompilerParams(vmem_limit_bytes=16 * MIB),
        cost_estimate=pl.CostEstimate(flops=2 * ROWS * COLS * 32, bytes_accessed=4 * ROWS * COLS, transcendentals=0),
        name="finish",
    )(merged, basis, inverse, right_sum, momentum)


def swap(x, axis, bit):
    return lax.ppermute(x, axis, [(i, i ^ bit) for i in range(lax.axis_size(axis))])


def shards(gradient, feedback, momentum, right_init):
    gradient = pltpu.with_memory_space_constraint(gradient, pltpu.HBM)
    feedback = pltpu.with_memory_space_constraint(feedback, pltpu.HBM)
    merged, keep, send = merge(gradient, feedback, right_init.T)
    own = keep + swap(send, "replica", 1)
    for axis, bit in (("replica", 2), ("replica", 4), ("tensor", 1), ("tensor", 2), ("tensor", 4), ("tensor", 8)):
        own = own + swap(own, axis, bit)
    other = swap(own, "replica", 1)
    right_sum = right_term(merged, own, other)
    inverse, basis = make_basis(own, other)
    for bit in (1, 2, 4):
        right_sum = right_sum + swap(right_sum, "replica", bit)
    feedback_out, momentum_out, right_t = finish(lax.axis_size("replica"), merged, basis, inverse, right_sum, momentum)
    return feedback_out, momentum_out, right_t.T


def solution(mesh):
    placed = (
        P("replica", None, "tensor"),
        P("replica", None, "tensor"),
        P("replica", "tensor"),
        P("tensor", None),
    )
    return jax.shard_map(
        shards,
        mesh=mesh,
        in_specs=placed,
        out_specs=(P("replica", None, "tensor"), P("replica", "tensor"), P("tensor", None)),
        check_vma=False,
    )
```

```python
import itertools

import jax
import jax.numpy as jnp
from jax import lax
from jax.experimental import pallas as pl
from jax.experimental.pallas import tpu as pltpu
from jax.sharding import PartitionSpec as P

F32, BF16 = jnp.float32, jnp.bfloat16
ROWS, COLS, RANK = 6144, 384, 8
HALF = ROWS // 2
CHUNKS = 6
CHUNK = ROWS // CHUNKS
MIB = 1 << 20


def own_half():
    replica, tensor = lax.axis_index("replica"), lax.axis_index("tensor")
    return lax.rem(replica + replica // 2 + tensor + tensor // 4, 2)


def split(x):
    high = x.astype(BF16)
    return high, (x - high.astype(F32)).astype(BF16)


def merge_kernel(g_ref, f_ref, q_ref, merged_ref, keep_ref, send_ref, g_buf, f_buf, q_buf, g_sem, f_sem, q_sem):
    q_copy = pltpu.make_async_copy(q_ref, q_buf, q_sem.at[0])
    q_copy.start()
    copies = []
    for i in range(CHUNKS):
        rows = pl.ds(i * CHUNK, CHUNK)
        pair = (
            pltpu.make_async_copy(g_ref.at[0, rows, :], g_buf.at[rows, :], g_sem.at[i]),
            pltpu.make_async_copy(f_ref.at[0, rows, :], f_buf.at[rows, :], f_sem.at[i]),
        )
        for copy in pair:
            copy.start()
        copies.append(pair)
    q_copy.wait()
    right = q_buf[...].astype(BF16)
    keep_first = own_half() == 0
    for i in range(CHUNKS):
        for copy in copies[i]:
            copy.wait()
        rows = pl.ds(i * CHUNK, CHUNK)
        merged = (g_buf[rows, :].astype(F32) + f_buf[rows, :].astype(F32)).astype(BF16)
        merged_ref[rows, :] = merged
        term = lax.dot_general(right, merged, (((1,), (1,)), ((), ())), preferred_element_type=F32)
        where = pl.ds(i % (CHUNKS // 2) * CHUNK, CHUNK)
        keep = keep_first if i < CHUNKS // 2 else jnp.logical_not(keep_first)

        @pl.when(keep)
        def _():
            keep_ref[:, where] = term

        @pl.when(jnp.logical_not(keep))
        def _():
            send_ref[:, where] = term


def whole():
    return pl.BlockSpec(memory_space=pltpu.VMEM)


def in_hbm(count):
    return [pl.BlockSpec(memory_space=pltpu.HBM)] * count


def merge(gradient, feedback, right_t):
    return pl.pallas_call(
        merge_kernel,
        in_specs=in_hbm(3),
        out_specs=[whole(), whole(), whole()],
        out_shape=[
            pltpu.VMEM((ROWS, COLS), BF16),
            pltpu.VMEM((RANK, HALF), F32),
            pltpu.VMEM((RANK, HALF), F32),
        ],
        scratch_shapes=[
            pltpu.VMEM((ROWS, COLS), BF16),
            pltpu.VMEM((ROWS, COLS), BF16),
            pltpu.VMEM((RANK, COLS), F32),
            pltpu.SemaphoreType.DMA((CHUNKS,)),
            pltpu.SemaphoreType.DMA((CHUNKS,)),
            pltpu.SemaphoreType.DMA((1,)),
        ],
        compiler_params=pltpu.CompilerParams(vmem_limit_bytes=20 * MIB),
        cost_estimate=pl.CostEstimate(flops=2 * ROWS * COLS * RANK, bytes_accessed=4 * ROWS * COLS, transcendentals=0),
        name="merge",
    )(gradient, feedback, right_t)


def right_kernel(merged_ref, own_ref, other_ref, out_ref):
    mine = own_half()
    total = jnp.zeros((2 * RANK, COLS), F32)
    for ref, half in ((own_ref, mine), (other_ref, 1 - mine)):
        rows = pl.ds(pl.multiple_of(half * HALF, HALF), HALF)
        pair = jnp.concatenate(split(ref[...]), axis=0)
        total += jnp.dot(pair, merged_ref[rows, :], preferred_element_type=F32)
    out_ref[...] = total[:RANK] + total[RANK:]


def right_term(merged, own, other):
    return pl.pallas_call(
        right_kernel,
        in_specs=[whole(), whole(), whole()],
        out_specs=whole(),
        out_shape=pltpu.VMEM((RANK, COLS), F32),
        compiler_params=pltpu.CompilerParams(vmem_limit_bytes=16 * MIB),
        cost_estimate=pl.CostEstimate(flops=4 * ROWS * COLS * RANK, bytes_accessed=2 * ROWS * COLS, transcendentals=0),
        name="right_term",
    )(merged, own, other)


def basis_kernel(own_ref, other_ref, inverse_ref, basis_ref):
    own, other = own_ref[...], other_ref[...]
    gram = jnp.zeros((RANK, RANK), F32)
    for part in (own, other):
        gram += lax.dot_general(
            part, part, (((1,), (1,)), ((), ())), precision=lax.Precision.HIGHEST, preferred_element_type=F32
        )
    row = lax.broadcasted_iota(jnp.int32, (RANK, RANK), 0)
    column = lax.broadcasted_iota(jnp.int32, (RANK, RANK), 1)
    eye = jnp.where(row == column, 1.0, 0.0)
    inverse = eye
    for k in range(RANK):
        factor = jnp.where(row[:, :1] > k, gram[:, k : k + 1] / gram[k : k + 1, k : k + 1], 0.0)
        inverse -= factor * inverse[k : k + 1, :]
        gram -= factor * gram[k : k + 1, :]
    pivots = jnp.sum(gram * eye, axis=1, keepdims=True)
    inverse = inverse / jnp.sqrt(pivots)
    inverse_ref[...] = inverse
    mine = own_half()
    for part, half in ((own, mine), (other, 1 - mine)):
        basis = jnp.zeros((RANK, HALF), F32)
        for k in range(RANK):
            basis += inverse[:, k : k + 1] * part[k : k + 1, :]
        high, low = split(basis)
        packed = jnp.concatenate([high, high, low, low], axis=0)
        basis_ref[pl.ds(pl.multiple_of(half * HALF, HALF), HALF), :] = packed.T


def make_basis(own, other):
    return pl.pallas_call(
        basis_kernel,
        in_specs=[whole(), whole()],
        out_specs=[whole(), whole()],
        out_shape=[pltpu.VMEM((RANK, RANK), F32), pltpu.VMEM((ROWS, 4 * RANK), BF16)],
        compiler_params=pltpu.CompilerParams(vmem_limit_bytes=16 * MIB),
        cost_estimate=pl.CostEstimate(flops=4 * ROWS * RANK * RANK, bytes_accessed=4 * MIB, transcendentals=0),
        name="basis",
    )(own, other)


def final_kernel(
    replicas,
    merged_ref, basis_ref, inverse_ref, sum_ref, last_ref, mom_ref,
    fb_ref, mom_out_ref, right_ref,
    fb_buf, mom_buf, right_buf, fb_sem, mom_sem, right_sem,
):
    total = sum_ref[...] + last_ref[...]
    right = jnp.zeros((RANK, COLS), F32)
    for k in range(RANK):
        right += inverse_ref[:, k : k + 1] * total[k : k + 1, :]
    right = right * (1.0 / replicas)
    right_buf[...] = right
    copies = [pltpu.make_async_copy(right_buf, right_ref, right_sem.at[0])]
    copies[0].start()
    high, low = split(right)
    pack = jnp.concatenate([high, low, high, low], axis=0)
    for i in range(CHUNKS):
        rows = pl.ds(i * CHUNK, CHUNK)
        approx = jnp.dot(basis_ref[rows, :], pack, preferred_element_type=F32)
        fb_buf[rows, :] = (merged_ref[rows, :].astype(F32) - approx).astype(BF16)
        copies.append(pltpu.make_async_copy(fb_buf.at[rows, :], fb_ref.at[0, rows, :], fb_sem.at[i]))
        copies[-1].start()
        if i == 0:
            count = mom_ref.shape[0]
            mom_rows = pl.ds(pl.multiple_of(lax.axis_index("replica") * count, count), count)
            approx = jnp.dot(basis_ref[mom_rows, :], pack, preferred_element_type=F32)
            mom_buf[...] = (0.9 * mom_ref[...].astype(F32) + approx).astype(BF16)
            copies.append(pltpu.make_async_copy(mom_buf, mom_out_ref, mom_sem.at[0]))
            copies[-1].start()
    for copy in copies:
        copy.wait()


def finish(replicas, merged, basis, inverse, right_sum, right_last, momentum):
    mom_rows = momentum.shape[0]

    def body(*refs):
        final_kernel(replicas, *refs)

    return pl.pallas_call(
        body,
        in_specs=[whole()] * 6,
        out_specs=in_hbm(3),
        out_shape=[
            jax.ShapeDtypeStruct((1, ROWS, COLS), BF16),
            jax.ShapeDtypeStruct((mom_rows, COLS), BF16),
            jax.ShapeDtypeStruct((RANK, COLS), F32),
        ],
        scratch_shapes=[
            pltpu.VMEM((ROWS, COLS), BF16),
            pltpu.VMEM((mom_rows, COLS), BF16),
            pltpu.VMEM((RANK, COLS), F32),
            pltpu.SemaphoreType.DMA((CHUNKS,)),
            pltpu.SemaphoreType.DMA((1,)),
            pltpu.SemaphoreType.DMA((1,)),
        ],
        compiler_params=pltpu.CompilerParams(vmem_limit_bytes=20 * MIB),
        cost_estimate=pl.CostEstimate(flops=2 * ROWS * COLS * 32, bytes_accessed=4 * ROWS * COLS, transcendentals=0),
        name="finish",
    )(merged, basis, inverse, right_sum, right_last, momentum)


NEAR = {0: 1, 1: 0, 2: 3, 3: 2}
WRAP = {0: 3, 3: 0, 1: 2, 2: 1}


def step_pairs(axes, partner):
    pairs = []
    for y, core, z, x in itertools.product(range(4), range(2), range(4), range(4)):
        here = {"y": y, "z": z, "x": x}
        axis = axes[(core + y + z + x) % 2]
        there = {**here, axis: partner[here[axis]]}
        place = lambda at, c: (2 * at["y"] + c) * 16 + 4 * at["z"] + at["x"]
        pairs.append((place(here, core), place(there, 1 - core)))
    return pairs


def step(x, axes, partner):
    return lax.ppermute(x, ("replica", "tensor"), step_pairs(axes, partner))


def sibling(x):
    return lax.ppermute(x, "replica", [(i, i ^ 1) for i in range(lax.axis_size("replica"))])


def shards(gradient, feedback, momentum, right_init):
    gradient = pltpu.with_memory_space_constraint(gradient, pltpu.HBM)
    feedback = pltpu.with_memory_space_constraint(feedback, pltpu.HBM)
    right_t = pltpu.with_memory_space_constraint(right_init.T, pltpu.HBM)
    momentum = pltpu.with_memory_space_constraint(momentum, pltpu.VMEM)
    merged, keep, send = merge(gradient, feedback, right_t)
    own = keep + sibling(send)
    for axes in ("yx", "xz", "zy"):
        for partner in (NEAR, WRAP):
            own = own + step(own, axes, partner)
    other = sibling(own)
    term = right_term(merged, own, other)
    inverse, basis = make_basis(own, other)
    term = term + sibling(term)
    term = term + step(term, "yy", NEAR)
    last = step(term, "yy", WRAP)
    feedback_out, momentum_out, right_t = finish(lax.axis_size("replica"), merged, basis, inverse, term, last, momentum)
    return feedback_out, momentum_out, right_t.T


def solution(mesh):
    placed = (
        P("replica", None, "tensor"),
        P("replica", None, "tensor"),
        P("replica", "tensor"),
        P("tensor", None),
    )
    return jax.shard_map(
        shards,
        mesh=mesh,
        in_specs=placed,
        out_specs=(P("replica", None, "tensor"), P("replica", "tensor"), P("tensor", None)),
        check_vma=False,
    )
```

```python
import itertools

import jax
import jax.numpy as jnp
from jax import lax
from jax.experimental import pallas as pl
from jax.experimental.pallas import tpu as pltpu
from jax.sharding import PartitionSpec as P

F32, BF16 = jnp.float32, jnp.bfloat16
ROWS, COLS, RANK = 6144, 384, 8
HALF = ROWS // 2
CHUNKS = 6
CHUNK = ROWS // CHUNKS
MIB = 1 << 20


def own_half():
    replica, tensor = lax.axis_index("replica"), lax.axis_index("tensor")
    return lax.rem(replica + replica // 2 + tensor + tensor // 4, 2)


def split(x):
    high = x.astype(BF16)
    return high, (x - high.astype(F32)).astype(BF16)


def merge_kernel(g_ref, f_ref, q_ref, merged_ref, keep_ref, send_ref, g_buf, f_buf, q_buf, g_sem, f_sem, q_sem):
    q_copy = pltpu.make_async_copy(q_ref, q_buf, q_sem.at[0])
    q_copy.start()
    copies = []
    for i in range(CHUNKS):
        rows = pl.ds(i * CHUNK, CHUNK)
        pair = (
            pltpu.make_async_copy(g_ref.at[0, rows, :], g_buf.at[rows, :], g_sem.at[i]),
            pltpu.make_async_copy(f_ref.at[0, rows, :], f_buf.at[rows, :], f_sem.at[i]),
        )
        for copy in pair:
            copy.start()
        copies.append(pair)
    q_copy.wait()
    right = q_buf[...].astype(BF16)
    keep_first = own_half() == 0
    for i in range(CHUNKS):
        for copy in copies[i]:
            copy.wait()
        rows = pl.ds(i * CHUNK, CHUNK)
        merged = (g_buf[rows, :].astype(F32) + f_buf[rows, :].astype(F32)).astype(BF16)
        merged_ref[rows, :] = merged
        term = lax.dot_general(right, merged, (((1,), (1,)), ((), ())), preferred_element_type=F32)
        where = pl.ds(i % (CHUNKS // 2) * CHUNK, CHUNK)
        keep = keep_first if i < CHUNKS // 2 else jnp.logical_not(keep_first)

        @pl.when(keep)
        def _():
            keep_ref[:, where] = term

        @pl.when(jnp.logical_not(keep))
        def _():
            send_ref[:, where] = term


def whole():
    return pl.BlockSpec(memory_space=pltpu.VMEM)


def in_hbm(count):
    return [pl.BlockSpec(memory_space=pltpu.HBM)] * count


def merge(gradient, feedback, right_t):
    return pl.pallas_call(
        merge_kernel,
        in_specs=in_hbm(3),
        out_specs=[whole(), whole(), whole()],
        out_shape=[
            pltpu.VMEM((ROWS, COLS), BF16),
            pltpu.VMEM((RANK, HALF), F32),
            pltpu.VMEM((RANK, HALF), F32),
        ],
        scratch_shapes=[
            pltpu.VMEM((ROWS, COLS), BF16),
            pltpu.VMEM((ROWS, COLS), BF16),
            pltpu.VMEM((RANK, COLS), F32),
            pltpu.SemaphoreType.DMA((CHUNKS,)),
            pltpu.SemaphoreType.DMA((CHUNKS,)),
            pltpu.SemaphoreType.DMA((1,)),
        ],
        compiler_params=pltpu.CompilerParams(vmem_limit_bytes=20 * MIB),
        cost_estimate=pl.CostEstimate(flops=2 * ROWS * COLS * RANK, bytes_accessed=4 * ROWS * COLS, transcendentals=0),
        name="merge",
    )(gradient, feedback, right_t)


def right_kernel(merged_ref, own_ref, other_ref, out_ref):
    mine = own_half()
    total = jnp.zeros((2 * RANK, COLS), F32)
    for ref, half in ((own_ref, mine), (other_ref, 1 - mine)):
        rows = pl.ds(pl.multiple_of(half * HALF, HALF), HALF)
        pair = jnp.concatenate(split(ref[...]), axis=0)
        total += jnp.dot(pair, merged_ref[rows, :], preferred_element_type=F32)
    out_ref[...] = total[:RANK] + total[RANK:]


def right_term(merged, own, other):
    return pl.pallas_call(
        right_kernel,
        in_specs=[whole(), whole(), whole()],
        out_specs=whole(),
        out_shape=pltpu.VMEM((RANK, COLS), F32),
        compiler_params=pltpu.CompilerParams(vmem_limit_bytes=16 * MIB),
        cost_estimate=pl.CostEstimate(flops=4 * ROWS * COLS * RANK, bytes_accessed=2 * ROWS * COLS, transcendentals=0),
        name="right_term",
    )(merged, own, other)


def basis_kernel(own_ref, other_ref, inverse_ref, basis_ref):
    own, other = own_ref[...], other_ref[...]
    gram = jnp.zeros((RANK, RANK), F32)
    for part in (own, other):
        gram += lax.dot_general(
            part, part, (((1,), (1,)), ((), ())), precision=lax.Precision.HIGHEST, preferred_element_type=F32
        )
    row = lax.broadcasted_iota(jnp.int32, (RANK, RANK), 0)
    column = lax.broadcasted_iota(jnp.int32, (RANK, RANK), 1)
    eye = jnp.where(row == column, 1.0, 0.0)
    inverse = eye
    for k in range(RANK):
        factor = jnp.where(row[:, :1] > k, gram[:, k : k + 1] / gram[k : k + 1, k : k + 1], 0.0)
        inverse -= factor * inverse[k : k + 1, :]
        gram -= factor * gram[k : k + 1, :]
    pivots = jnp.sum(gram * eye, axis=1, keepdims=True)
    inverse = inverse / jnp.sqrt(pivots)
    inverse_ref[...] = inverse
    mine = own_half()
    for part, half in ((own, mine), (other, 1 - mine)):
        basis = jnp.zeros((RANK, HALF), F32)
        for k in range(RANK):
            basis += inverse[:, k : k + 1] * part[k : k + 1, :]
        high, low = split(basis)
        packed = jnp.concatenate([high, high, low, low], axis=0)
        basis_ref[pl.ds(pl.multiple_of(half * HALF, HALF), HALF), :] = packed.T


def make_basis(own, other):
    return pl.pallas_call(
        basis_kernel,
        in_specs=[whole(), whole()],
        out_specs=[whole(), whole()],
        out_shape=[pltpu.VMEM((RANK, RANK), F32), pltpu.VMEM((ROWS, 4 * RANK), BF16)],
        compiler_params=pltpu.CompilerParams(vmem_limit_bytes=16 * MIB),
        cost_estimate=pl.CostEstimate(flops=4 * ROWS * RANK * RANK, bytes_accessed=4 * MIB, transcendentals=0),
        name="basis",
    )(own, other)


def final_kernel(
    replicas,
    merged_ref, basis_ref, inverse_ref, sum_ref, near_ref, wrap_ref, far_ref, mom_ref,
    fb_ref, mom_out_ref, right_ref,
    fb_buf, mom_buf, right_buf, fb_sem, mom_sem, right_sem,
):
    total = (sum_ref[...] + near_ref[...]) + (wrap_ref[...] + far_ref[...])
    right = jnp.zeros((RANK, COLS), F32)
    for k in range(RANK):
        right += inverse_ref[:, k : k + 1] * total[k : k + 1, :]
    right = right * (1.0 / replicas)
    right_buf[...] = right
    copies = [pltpu.make_async_copy(right_buf, right_ref, right_sem.at[0])]
    copies[0].start()
    high, low = split(right)
    pack = jnp.concatenate([high, low, high, low], axis=0)
    for i in range(CHUNKS):
        rows = pl.ds(i * CHUNK, CHUNK)
        approx = jnp.dot(basis_ref[rows, :], pack, preferred_element_type=F32)
        fb_buf[rows, :] = (merged_ref[rows, :].astype(F32) - approx).astype(BF16)
        copies.append(pltpu.make_async_copy(fb_buf.at[rows, :], fb_ref.at[0, rows, :], fb_sem.at[i]))
        copies[-1].start()
        if i == 0:
            count = mom_ref.shape[0]
            mom_rows = pl.ds(pl.multiple_of(lax.axis_index("replica") * count, count), count)
            approx = jnp.dot(basis_ref[mom_rows, :], pack, preferred_element_type=F32)
            mom_buf[...] = (0.9 * mom_ref[...].astype(F32) + approx).astype(BF16)
            copies.append(pltpu.make_async_copy(mom_buf, mom_out_ref, mom_sem.at[0]))
            copies[-1].start()
    for copy in copies:
        copy.wait()


def finish(replicas, merged, basis, inverse, parts, momentum):
    mom_rows = momentum.shape[0]

    def body(*refs):
        final_kernel(replicas, *refs)

    return pl.pallas_call(
        body,
        in_specs=[whole()] * 8,
        out_specs=in_hbm(3),
        out_shape=[
            jax.ShapeDtypeStruct((1, ROWS, COLS), BF16),
            jax.ShapeDtypeStruct((mom_rows, COLS), BF16),
            jax.ShapeDtypeStruct((RANK, COLS), F32),
        ],
        scratch_shapes=[
            pltpu.VMEM((ROWS, COLS), BF16),
            pltpu.VMEM((mom_rows, COLS), BF16),
            pltpu.VMEM((RANK, COLS), F32),
            pltpu.SemaphoreType.DMA((CHUNKS,)),
            pltpu.SemaphoreType.DMA((1,)),
            pltpu.SemaphoreType.DMA((1,)),
        ],
        compiler_params=pltpu.CompilerParams(vmem_limit_bytes=20 * MIB),
        cost_estimate=pl.CostEstimate(flops=2 * ROWS * COLS * 32, bytes_accessed=4 * ROWS * COLS, transcendentals=0),
        name="finish",
    )(merged, basis, inverse, *parts, momentum)


def step_pairs(axes, flip, swap_cores):
    pairs = []
    for y, core, z, x in itertools.product(range(4), range(2), range(4), range(4)):
        here = {"y": y, "z": z, "x": x}
        axis = axes[(core + y + z + x) % 2]
        there = {**here, axis: here[axis] ^ flip}
        place = lambda at, c: (2 * at["y"] + c) * 16 + 4 * at["z"] + at["x"]
        pairs.append((place(here, core), place(there, core ^ swap_cores)))
    return pairs


def ring(x, axes, far_swap):
    steps = ((1, 1), (3, 1), (2, far_swap))
    return [lax.ppermute(x, ("replica", "tensor"), step_pairs(axes, *s)) for s in steps]


def sibling(x):
    return lax.ppermute(x, "replica", [(i, i ^ 1) for i in range(lax.axis_size("replica"))])


def shards(gradient, feedback, momentum, right_init):
    gradient = pltpu.with_memory_space_constraint(gradient, pltpu.HBM)
    feedback = pltpu.with_memory_space_constraint(feedback, pltpu.HBM)
    right_t = pltpu.with_memory_space_constraint(right_init.T, pltpu.HBM)
    momentum = pltpu.with_memory_space_constraint(momentum, pltpu.VMEM)
    merged, keep, send = merge(gradient, feedback, right_t)
    own = keep + sibling(send)
    for axes in ("yx", "xz", "zy"):
        near, wrap, far = ring(own, axes, 0)
        own = own + near + wrap + far
    other = sibling(own)
    term = right_term(merged, own, other)
    inverse, basis = make_basis(own, other)
    term = term + sibling(term)
    parts = [term, *ring(term, "yy", 1)]
    feedback_out, momentum_out, right_t = finish(lax.axis_size("replica"), merged, basis, inverse, parts, momentum)
    return feedback_out, momentum_out, right_t.T


def solution(mesh):
    placed = (
        P("replica", None, "tensor"),
        P("replica", None, "tensor"),
        P("replica", "tensor"),
        P("tensor", None),
    )
    return jax.shard_map(
        shards,
        mesh=mesh,
        in_specs=placed,
        out_specs=(P("replica", None, "tensor"), P("replica", "tensor"), P("tensor", None)),
        check_vma=False,
    )
```

```python
import itertools

import jax
import jax.numpy as jnp
from jax import lax
from jax.experimental import pallas as pl
from jax.experimental.pallas import tpu as pltpu
from jax.sharding import PartitionSpec as P

F32, BF16 = jnp.float32, jnp.bfloat16
ROWS, COLS, RANK = 6144, 384, 8
HALF = ROWS // 2
CHUNKS = 3
CHUNK = HALF // CHUNKS
MIB = 1 << 20


def own_half():
    replica, tensor = lax.axis_index("replica"), lax.axis_index("tensor")
    return lax.rem(replica + replica // 2 + tensor + tensor // 4, 2)


def split(x):
    high = x.astype(BF16)
    return high, (x - high.astype(F32)).astype(BF16)


def rows_of(half, chunk):
    return pl.ds(pl.multiple_of(half * HALF + chunk * CHUNK, CHUNK), CHUNK)


def merge_kernel(mine, g_ref, f_ref, q_ref, merged_ref, term_ref, g_buf, f_buf, q_buf, g_sem, f_sem, q_sem):
    half = own_half() if mine else 1 - own_half()
    q_copy = pltpu.make_async_copy(q_ref, q_buf, q_sem.at[0])
    q_copy.start()
    copies = []
    for i in range(CHUNKS):
        here = pl.ds(i * CHUNK, CHUNK)
        pair = (
            pltpu.make_async_copy(g_ref.at[0, rows_of(half, i), :], g_buf.at[here, :], g_sem.at[i]),
            pltpu.make_async_copy(f_ref.at[0, rows_of(half, i), :], f_buf.at[here, :], f_sem.at[i]),
        )
        for copy in pair:
            copy.start()
        copies.append(pair)
    q_copy.wait()
    right = q_buf[...].astype(BF16)
    for i in range(CHUNKS):
        for copy in copies[i]:
            copy.wait()
        here = pl.ds(i * CHUNK, CHUNK)
        merged = (g_buf[here, :].astype(F32) + f_buf[here, :].astype(F32)).astype(BF16)
        merged_ref[here, :] = merged
        term_ref[:, here] = lax.dot_general(
            right, merged, (((1,), (1,)), ((), ())), preferred_element_type=F32
        )


def whole():
    return pl.BlockSpec(memory_space=pltpu.VMEM)


def in_hbm(count):
    return [pl.BlockSpec(memory_space=pltpu.HBM)] * count


def merge(mine, gradient, feedback, right_t):
    def body(*refs):
        merge_kernel(mine, *refs)

    return pl.pallas_call(
        body,
        in_specs=in_hbm(3),
        out_specs=[whole(), whole()],
        out_shape=[pltpu.VMEM((HALF, COLS), BF16), pltpu.VMEM((RANK, HALF), F32)],
        scratch_shapes=[
            pltpu.VMEM((HALF, COLS), BF16),
            pltpu.VMEM((HALF, COLS), BF16),
            pltpu.VMEM((RANK, COLS), F32),
            pltpu.SemaphoreType.DMA((CHUNKS,)),
            pltpu.SemaphoreType.DMA((CHUNKS,)),
            pltpu.SemaphoreType.DMA((1,)),
        ],
        compiler_params=pltpu.CompilerParams(vmem_limit_bytes=16 * MIB),
        cost_estimate=pl.CostEstimate(flops=HALF * COLS * RANK * 2, bytes_accessed=4 * HALF * COLS, transcendentals=0),
        name="merge_own" if mine else "merge_other",
    )(gradient, feedback, right_t)


def right_kernel(merged_ref, left_ref, *refs):
    pair = jnp.concatenate(split(left_ref[...]), axis=0)
    total = jnp.dot(pair, merged_ref[...], preferred_element_type=F32)
    total = total[:RANK] + total[RANK:]
    for ref in refs[:-1]:
        total += ref[...]
    refs[-1][...] = total


def right_term(merged, left, *before):
    return pl.pallas_call(
        right_kernel,
        in_specs=[whole()] * (2 + len(before)),
        out_specs=whole(),
        out_shape=pltpu.VMEM((RANK, COLS), F32),
        compiler_params=pltpu.CompilerParams(vmem_limit_bytes=16 * MIB),
        cost_estimate=pl.CostEstimate(flops=4 * HALF * COLS * RANK, bytes_accessed=2 * HALF * COLS, transcendentals=0),
        name="right_other" if before else "right_own",
    )(merged, left, *before)


def basis_kernel(own_ref, other_ref, inverse_ref, basis_ref):
    own, other = own_ref[...], other_ref[...]
    gram = jnp.zeros((RANK, RANK), F32)
    for part in (own, other):
        gram += lax.dot_general(
            part, part, (((1,), (1,)), ((), ())), precision=lax.Precision.HIGHEST, preferred_element_type=F32
        )
    row = lax.broadcasted_iota(jnp.int32, (RANK, RANK), 0)
    column = lax.broadcasted_iota(jnp.int32, (RANK, RANK), 1)
    eye = jnp.where(row == column, 1.0, 0.0)
    inverse = eye
    for k in range(RANK):
        factor = jnp.where(row[:, :1] > k, gram[:, k : k + 1] / gram[k : k + 1, k : k + 1], 0.0)
        inverse -= factor * inverse[k : k + 1, :]
        gram -= factor * gram[k : k + 1, :]
    pivots = jnp.sum(gram * eye, axis=1, keepdims=True)
    inverse = inverse / jnp.sqrt(pivots)
    inverse_ref[...] = inverse
    for part, start in ((own, 0), (other, HALF)):
        basis = jnp.zeros((RANK, HALF), F32)
        for k in range(RANK):
            basis += inverse[:, k : k + 1] * part[k : k + 1, :]
        high, low = split(basis)
        packed = jnp.concatenate([high, high, low, low], axis=0)
        basis_ref[start : start + HALF, :] = packed.T


def make_basis(own, other):
    return pl.pallas_call(
        basis_kernel,
        in_specs=[whole(), whole()],
        out_specs=[whole(), whole()],
        out_shape=[pltpu.VMEM((RANK, RANK), F32), pltpu.VMEM((ROWS, 4 * RANK), BF16)],
        compiler_params=pltpu.CompilerParams(vmem_limit_bytes=16 * MIB),
        cost_estimate=pl.CostEstimate(flops=4 * ROWS * RANK * RANK, bytes_accessed=4 * MIB, transcendentals=0),
        name="basis",
    )(own, other)


def final_kernel(
    replicas,
    own_ref, other_ref, basis_ref, inverse_ref, sum_ref, near_ref, wrap_ref, far_ref, mom_ref,
    fb_ref, mom_out_ref, right_ref,
    fb_buf, mom_buf, right_buf, fb_sem, mom_sem, right_sem,
):
    total = (sum_ref[...] + near_ref[...]) + (wrap_ref[...] + far_ref[...])
    right = jnp.zeros((RANK, COLS), F32)
    for k in range(RANK):
        right += inverse_ref[:, k : k + 1] * total[k : k + 1, :]
    right = right * (1.0 / replicas)
    right_buf[...] = right
    copies = [pltpu.make_async_copy(right_buf, right_ref, right_sem.at[0])]
    copies[0].start()
    high, low = split(right)
    pack = jnp.concatenate([high, low, high, low], axis=0)
    mine = own_half()
    for i in range(2 * CHUNKS):
        rows = pl.ds(i * CHUNK, CHUNK)
        merged_ref, half = (own_ref, mine) if i < CHUNKS else (other_ref, 1 - mine)
        merged = merged_ref[pl.ds(i % CHUNKS * CHUNK, CHUNK), :]
        approx = jnp.dot(basis_ref[rows, :], pack, preferred_element_type=F32)
        fb_buf[rows, :] = (merged.astype(F32) - approx).astype(BF16)
        target = fb_ref.at[0, rows_of(half, i % CHUNKS), :]
        copies.append(pltpu.make_async_copy(fb_buf.at[rows, :], target, fb_sem.at[i]))
        copies[-1].start()
        if i == 0:
            count = mom_ref.shape[0]
            replica, per_half = lax.axis_index("replica"), HALF // count
            start = jnp.where(replica // per_half == mine, 0, HALF) + lax.rem(replica, per_half) * count
            mom_rows = pl.ds(pl.multiple_of(start, count), count)
            approx = jnp.dot(basis_ref[mom_rows, :], pack, preferred_element_type=F32)
            mom_buf[...] = (0.9 * mom_ref[...].astype(F32) + approx).astype(BF16)
            copies.append(pltpu.make_async_copy(mom_buf, mom_out_ref, mom_sem.at[0]))
            copies[-1].start()
    for copy in copies:
        copy.wait()


def finish(replicas, merged_own, merged_other, basis, inverse, parts, momentum):
    mom_rows = momentum.shape[0]

    def body(*refs):
        final_kernel(replicas, *refs)

    return pl.pallas_call(
        body,
        in_specs=[whole()] * 9,
        out_specs=in_hbm(3),
        out_shape=[
            jax.ShapeDtypeStruct((1, ROWS, COLS), BF16),
            jax.ShapeDtypeStruct((mom_rows, COLS), BF16),
            jax.ShapeDtypeStruct((RANK, COLS), F32),
        ],
        scratch_shapes=[
            pltpu.VMEM((ROWS, COLS), BF16),
            pltpu.VMEM((mom_rows, COLS), BF16),
            pltpu.VMEM((RANK, COLS), F32),
            pltpu.SemaphoreType.DMA((2 * CHUNKS,)),
            pltpu.SemaphoreType.DMA((1,)),
            pltpu.SemaphoreType.DMA((1,)),
        ],
        compiler_params=pltpu.CompilerParams(vmem_limit_bytes=20 * MIB),
        cost_estimate=pl.CostEstimate(flops=2 * ROWS * COLS * 32, bytes_accessed=4 * ROWS * COLS, transcendentals=0),
        name="finish",
    )(merged_own, merged_other, basis, inverse, *parts, momentum)


def step_pairs(axes, flip, swap_cores):
    pairs = []
    for y, core, z, x in itertools.product(range(4), range(2), range(4), range(4)):
        here = {"y": y, "z": z, "x": x}
        axis = axes[(core + y + z + x) % 2]
        there = {**here, axis: here[axis] ^ flip}
        place = lambda at, c: (2 * at["y"] + c) * 16 + 4 * at["z"] + at["x"]
        pairs.append((place(here, core), place(there, core ^ swap_cores)))
    return pairs


def ring(x, axes, far_swap):
    steps = ((1, 1), (3, 1), (2, far_swap))
    return [lax.ppermute(x, ("replica", "tensor"), step_pairs(axes, *s)) for s in steps]


def sibling(x):
    return lax.ppermute(x, "replica", [(i, i ^ 1) for i in range(lax.axis_size("replica"))])


def shards(gradient, feedback, momentum, right_init):
    gradient = pltpu.with_memory_space_constraint(gradient, pltpu.HBM)
    feedback = pltpu.with_memory_space_constraint(feedback, pltpu.HBM)
    right_t = pltpu.with_memory_space_constraint(right_init.T, pltpu.HBM)
    momentum = pltpu.with_memory_space_constraint(momentum, pltpu.VMEM)
    merged_other, send = merge(False, gradient, feedback, right_t)
    received = sibling(send)
    merged_own, keep = merge(True, gradient, feedback, right_t)
    own = keep + received
    for axes in ("yx", "xz", "zy"):
        near, wrap, far = ring(own, axes, 0)
        own = own + near + wrap + far
    other = sibling(own)
    term = right_term(merged_other, other, right_term(merged_own, own))
    inverse, basis = make_basis(own, other)
    term = term + sibling(term)
    parts = [term, *ring(term, "yy", 1)]
    feedback_out, momentum_out, right_t = finish(
        lax.axis_size("replica"), merged_own, merged_other, basis, inverse, parts, momentum
    )
    return feedback_out, momentum_out, right_t.T


def solution(mesh):
    placed = (
        P("replica", None, "tensor"),
        P("replica", None, "tensor"),
        P("replica", "tensor"),
        P("tensor", None),
    )
    return jax.shard_map(
        shards,
        mesh=mesh,
        in_specs=placed,
        out_specs=(P("replica", None, "tensor"), P("replica", "tensor"), P("tensor", None)),
        check_vma=False,
    )
```

```python
import itertools

import jax
import jax.numpy as jnp
from jax import lax
from jax.experimental import pallas as pl
from jax.experimental.pallas import tpu as pltpu
from jax.sharding import PartitionSpec as P

F32, BF16 = jnp.float32, jnp.bfloat16
ROWS, COLS, RANK = 6144, 384, 8
HALF = ROWS // 2
CHUNKS = 3
CHUNK = HALF // CHUNKS
MIB = 1 << 20


def own_half():
    replica, tensor = lax.axis_index("replica"), lax.axis_index("tensor")
    return lax.rem(replica + replica // 2 + tensor + tensor // 4, 2)


def split(x):
    high = x.astype(BF16)
    return high, (x - high.astype(F32)).astype(BF16)


def rows_of(half, chunk):
    return pl.ds(pl.multiple_of(half * HALF + chunk * CHUNK, CHUNK), CHUNK)


def merge_chunk(g_ref, f_ref, right, merged_ref, term_ref, i):
    here = pl.ds(i * CHUNK, CHUNK)
    merged = (g_ref[here, :].astype(F32) + f_ref[here, :].astype(F32)).astype(BF16)
    merged_ref[here, :] = merged
    term_ref[:, here] = lax.dot_general(right, merged, (((1,), (1,)), ((), ())), preferred_element_type=F32)


def load_kernel(g_ref, f_ref, q_ref, merged_ref, term_ref, g_own, f_own, q_own, g_buf, f_buf, g_sem, f_sem, q_sem):
    mine = own_half()
    q_copy = pltpu.make_async_copy(q_ref, q_own, q_sem.at[0])
    q_copy.start()
    copies = []
    for half, g_to, f_to in ((1 - mine, g_buf, f_buf), (mine, g_own, f_own)):
        for i in range(CHUNKS):
            here, n = pl.ds(i * CHUNK, CHUNK), len(copies)
            pair = (
                pltpu.make_async_copy(g_ref.at[0, rows_of(half, i), :], g_to.at[here, :], g_sem.at[n]),
                pltpu.make_async_copy(f_ref.at[0, rows_of(half, i), :], f_to.at[here, :], f_sem.at[n]),
            )
            for copy in pair:
                copy.start()
            copies.append(pair)
    q_copy.wait()
    right = q_own[...].astype(BF16)
    for i in range(2 * CHUNKS):
        for copy in copies[i]:
            copy.wait()
        if i < CHUNKS:
            merge_chunk(g_buf, f_buf, right, merged_ref, term_ref, i)


def merge_kernel(g_ref, f_ref, q_ref, merged_ref, term_ref):
    right = q_ref[...].astype(BF16)
    for i in range(CHUNKS):
        merge_chunk(g_ref, f_ref, right, merged_ref, term_ref, i)


def whole():
    return pl.BlockSpec(memory_space=pltpu.VMEM)


def in_hbm(count):
    return [pl.BlockSpec(memory_space=pltpu.HBM)] * count


def merge_other(gradient, feedback, right_t):
    half_rows = pltpu.VMEM((HALF, COLS), BF16)
    return pl.pallas_call(
        load_kernel,
        in_specs=in_hbm(3),
        out_specs=[whole()] * 5,
        out_shape=[half_rows, pltpu.VMEM((RANK, HALF), F32), half_rows, half_rows, pltpu.VMEM((RANK, COLS), F32)],
        scratch_shapes=[
            half_rows,
            half_rows,
            pltpu.SemaphoreType.DMA((2 * CHUNKS,)),
            pltpu.SemaphoreType.DMA((2 * CHUNKS,)),
            pltpu.SemaphoreType.DMA((1,)),
        ],
        compiler_params=pltpu.CompilerParams(vmem_limit_bytes=16 * MIB),
        cost_estimate=pl.CostEstimate(flops=HALF * COLS * RANK * 2, bytes_accessed=8 * HALF * COLS, transcendentals=0),
        name="merge_other",
    )(gradient, feedback, right_t)


def merge_own(gradient, feedback, right_t):
    return pl.pallas_call(
        merge_kernel,
        in_specs=[whole()] * 3,
        out_specs=[whole(), whole()],
        out_shape=[pltpu.VMEM((HALF, COLS), BF16), pltpu.VMEM((RANK, HALF), F32)],
        compiler_params=pltpu.CompilerParams(vmem_limit_bytes=16 * MIB),
        cost_estimate=pl.CostEstimate(flops=HALF * COLS * RANK * 2, bytes_accessed=4 * HALF * COLS, transcendentals=0),
        name="merge_own",
    )(gradient, feedback, right_t)


def right_kernel(merged_ref, left_ref, *refs):
    pair = jnp.concatenate(split(left_ref[...]), axis=0)
    total = jnp.dot(pair, merged_ref[...], preferred_element_type=F32)
    total = total[:RANK] + total[RANK:]
    for ref in refs[:-1]:
        total += ref[...]
    refs[-1][...] = total


def right_term(merged, left, *before):
    return pl.pallas_call(
        right_kernel,
        in_specs=[whole()] * (2 + len(before)),
        out_specs=whole(),
        out_shape=pltpu.VMEM((RANK, COLS), F32),
        compiler_params=pltpu.CompilerParams(vmem_limit_bytes=16 * MIB),
        cost_estimate=pl.CostEstimate(flops=4 * HALF * COLS * RANK, bytes_accessed=2 * HALF * COLS, transcendentals=0),
        name="right_other" if before else "right_own",
    )(merged, left, *before)


def basis_kernel(own_ref, other_ref, inverse_ref, basis_ref):
    own, other = own_ref[...], other_ref[...]
    gram = jnp.zeros((RANK, RANK), F32)
    for part in (own, other):
        gram += lax.dot_general(
            part, part, (((1,), (1,)), ((), ())), precision=lax.Precision.HIGHEST, preferred_element_type=F32
        )
    row = lax.broadcasted_iota(jnp.int32, (RANK, RANK), 0)
    column = lax.broadcasted_iota(jnp.int32, (RANK, RANK), 1)
    eye = jnp.where(row == column, 1.0, 0.0)
    inverse = eye
    for k in range(RANK):
        factor = jnp.where(row[:, :1] > k, gram[:, k : k + 1] / gram[k : k + 1, k : k + 1], 0.0)
        inverse -= factor * inverse[k : k + 1, :]
        gram -= factor * gram[k : k + 1, :]
    pivots = jnp.sum(gram * eye, axis=1, keepdims=True)
    inverse = inverse / jnp.sqrt(pivots)
    inverse_ref[...] = inverse
    for part, start in ((own, 0), (other, HALF)):
        basis = jnp.zeros((RANK, HALF), F32)
        for k in range(RANK):
            basis += inverse[:, k : k + 1] * part[k : k + 1, :]
        high, low = split(basis)
        packed = jnp.concatenate([high, high, low, low], axis=0)
        basis_ref[start : start + HALF, :] = packed.T


def make_basis(own, other):
    return pl.pallas_call(
        basis_kernel,
        in_specs=[whole(), whole()],
        out_specs=[whole(), whole()],
        out_shape=[pltpu.VMEM((RANK, RANK), F32), pltpu.VMEM((ROWS, 4 * RANK), BF16)],
        compiler_params=pltpu.CompilerParams(vmem_limit_bytes=16 * MIB),
        cost_estimate=pl.CostEstimate(flops=4 * ROWS * RANK * RANK, bytes_accessed=4 * MIB, transcendentals=0),
        name="basis",
    )(own, other)


def final_kernel(
    replicas,
    own_ref, other_ref, basis_ref, inverse_ref, sum_ref, near_ref, wrap_ref, far_ref, mom_ref,
    fb_ref, mom_out_ref, right_ref,
    fb_buf, mom_buf, right_buf, fb_sem, mom_sem, right_sem,
):
    total = (sum_ref[...] + near_ref[...]) + (wrap_ref[...] + far_ref[...])
    right = jnp.zeros((RANK, COLS), F32)
    for k in range(RANK):
        right += inverse_ref[:, k : k + 1] * total[k : k + 1, :]
    right = right * (1.0 / replicas)
    right_buf[...] = right
    copies = [pltpu.make_async_copy(right_buf, right_ref, right_sem.at[0])]
    copies[0].start()
    high, low = split(right)
    pack = jnp.concatenate([high, low, high, low], axis=0)
    mine = own_half()
    for i in range(2 * CHUNKS):
        rows = pl.ds(i * CHUNK, CHUNK)
        merged_ref, half = (own_ref, mine) if i < CHUNKS else (other_ref, 1 - mine)
        merged = merged_ref[pl.ds(i % CHUNKS * CHUNK, CHUNK), :]
        approx = jnp.dot(basis_ref[rows, :], pack, preferred_element_type=F32)
        fb_buf[rows, :] = (merged.astype(F32) - approx).astype(BF16)
        target = fb_ref.at[0, rows_of(half, i % CHUNKS), :]
        copies.append(pltpu.make_async_copy(fb_buf.at[rows, :], target, fb_sem.at[i]))
        copies[-1].start()
        if i == 0:
            count = mom_ref.shape[0]
            replica, per_half = lax.axis_index("replica"), HALF // count
            start = jnp.where(replica // per_half == mine, 0, HALF) + lax.rem(replica, per_half) * count
            mom_rows = pl.ds(pl.multiple_of(start, count), count)
            approx = jnp.dot(basis_ref[mom_rows, :], pack, preferred_element_type=F32)
            mom_buf[...] = (0.9 * mom_ref[...].astype(F32) + approx).astype(BF16)
            copies.append(pltpu.make_async_copy(mom_buf, mom_out_ref, mom_sem.at[0]))
            copies[-1].start()
    for copy in copies:
        copy.wait()


def finish(replicas, merged_own, merged_other, basis, inverse, parts, momentum):
    mom_rows = momentum.shape[0]

    def body(*refs):
        final_kernel(replicas, *refs)

    return pl.pallas_call(
        body,
        in_specs=[whole()] * 9,
        out_specs=in_hbm(3),
        out_shape=[
            jax.ShapeDtypeStruct((1, ROWS, COLS), BF16),
            jax.ShapeDtypeStruct((mom_rows, COLS), BF16),
            jax.ShapeDtypeStruct((RANK, COLS), F32),
        ],
        scratch_shapes=[
            pltpu.VMEM((ROWS, COLS), BF16),
            pltpu.VMEM((mom_rows, COLS), BF16),
            pltpu.VMEM((RANK, COLS), F32),
            pltpu.SemaphoreType.DMA((2 * CHUNKS,)),
            pltpu.SemaphoreType.DMA((1,)),
            pltpu.SemaphoreType.DMA((1,)),
        ],
        compiler_params=pltpu.CompilerParams(vmem_limit_bytes=20 * MIB),
        cost_estimate=pl.CostEstimate(flops=2 * ROWS * COLS * 32, bytes_accessed=4 * ROWS * COLS, transcendentals=0),
        name="finish",
    )(merged_own, merged_other, basis, inverse, *parts, momentum)


FLIP = {"n": 1, "w": 3, "f": 2}


def move_pairs(moves, swap):
    pairs = []
    for y, core, z, x in itertools.product(range(4), range(2), range(4), range(4)):
        there = {"y": y, "z": z, "x": x}
        for kind, axis in moves[(core + y + z + x) % 2]:
            there[axis] ^= FLIP[kind]
        to = 2 * there["y"] + (core ^ swap)
        pairs.append((16 * (2 * y + core) + 4 * z + x, 16 * to + 4 * there["z"] + there["x"]))
    return pairs


def move(x, moves, swap):
    return lax.ppermute(x, ("replica", "tensor"), move_pairs(moves, swap))


def group_sum(x, first, second):
    both = [[a, b] for a, b in zip(first, second)]
    near = move(x, [[a] for a in first], 1)
    wrap = move(x, [[b] for b in second], 1)
    return x + near + wrap + move(x, both, 0)


def sibling(x):
    return lax.ppermute(x, "replica", [(i, i ^ 1) for i in range(lax.axis_size("replica"))])


def shards(gradient, feedback, momentum, right_init):
    gradient = pltpu.with_memory_space_constraint(gradient, pltpu.HBM)
    feedback = pltpu.with_memory_space_constraint(feedback, pltpu.HBM)
    right_t = pltpu.with_memory_space_constraint(right_init.T, pltpu.HBM)
    momentum = pltpu.with_memory_space_constraint(momentum, pltpu.VMEM)
    merged_other, send, *loaded = merge_other(gradient, feedback, right_t)
    received = sibling(send)
    merged_own, keep = merge_own(*loaded)
    own = keep + received
    own = group_sum(own, ("ny", "nx"), ("wx", "wy"))
    own = group_sum(own, ("nz", "ny"), ("wy", "wz"))
    own = group_sum(own, ("nx", "nz"), ("wz", "wx"))
    other = sibling(own)
    term = right_term(merged_other, other, right_term(merged_own, own))
    inverse, basis = make_basis(own, other)
    term = term + sibling(term)
    parts = [term, *(move(term, [[kind]] * 2, 1) for kind in ("ny", "wy", "fy"))]
    feedback_out, momentum_out, right_t = finish(
        lax.axis_size("replica"), merged_own, merged_other, basis, inverse, parts, momentum
    )
    return feedback_out, momentum_out, right_t.T


def solution(mesh):
    placed = (
        P("replica", None, "tensor"),
        P("replica", None, "tensor"),
        P("replica", "tensor"),
        P("tensor", None),
    )
    return jax.shard_map(
        shards,
        mesh=mesh,
        in_specs=placed,
        out_specs=(P("replica", None, "tensor"), P("replica", "tensor"), P("tensor", None)),
        check_vma=False,
    )
```

```python
import itertools

import jax
import jax.numpy as jnp
from jax import lax
from jax.experimental import pallas as pl
from jax.experimental.pallas import tpu as pltpu
from jax.sharding import PartitionSpec as P

F32, BF16 = jnp.float32, jnp.bfloat16
ROWS, COLS, RANK = 6144, 384, 8
HALF = ROWS // 2
CHUNKS = 3
CHUNK = HALF // CHUNKS
MIB = 1 << 20


def own_half():
    replica, tensor = lax.axis_index("replica"), lax.axis_index("tensor")
    return lax.rem(replica + replica // 2 + tensor + tensor // 4, 2)


def split(x):
    high = x.astype(BF16)
    return high, (x - high.astype(F32)).astype(BF16)


def rows_of(half, chunk):
    return pl.ds(pl.multiple_of(half * HALF + chunk * CHUNK, CHUNK), CHUNK)


def merge_chunk(g_ref, f_ref, right, merged_ref, term_ref, i):
    here = pl.ds(i * CHUNK, CHUNK)
    merged = (g_ref[here, :].astype(F32) + f_ref[here, :].astype(F32)).astype(BF16)
    merged_ref[here, :] = merged
    term_ref[:, here] = lax.dot_general(right, merged, (((1,), (1,)), ((), ())), preferred_element_type=F32)


def load_pair(g_ref, f_ref, half, i, g_to, f_to, g_sem, f_sem):
    here = pl.ds(i * CHUNK, CHUNK)
    pair = (
        pltpu.make_async_copy(g_ref.at[0, rows_of(half, i), :], g_to.at[here, :], g_sem),
        pltpu.make_async_copy(f_ref.at[0, rows_of(half, i), :], f_to.at[here, :], f_sem),
    )
    for copy in pair:
        copy.start()
    return pair


def load_kernel(g_ref, f_ref, q_ref, merged_ref, term_ref, g_own, f_own, q_own, g_buf, f_buf, g_sem, f_sem, q_sem):
    mine = own_half()
    q_copy = pltpu.make_async_copy(q_ref, q_own, q_sem.at[0])
    q_copy.start()
    copies = []
    for half, g_to, f_to, count in ((1 - mine, g_buf, f_buf, CHUNKS), (mine, g_own, f_own, CHUNKS - 1)):
        for i in range(count):
            n = len(copies)
            copies.append(load_pair(g_ref, f_ref, half, i, g_to, f_to, g_sem.at[n], f_sem.at[n]))
    q_copy.wait()
    right = q_own[...].astype(BF16)
    for i, pair in enumerate(copies):
        for copy in pair:
            copy.wait()
        if i < CHUNKS:
            merge_chunk(g_buf, f_buf, right, merged_ref, term_ref, i)


def merge_kernel(g_ref, f_ref, g_own, f_own, q_ref, merged_ref, term_ref, g_buf, f_buf, g_sem, f_sem):
    last = CHUNKS - 1
    pair = load_pair(g_ref, f_ref, own_half(), last, g_buf, f_buf, g_sem.at[0], f_sem.at[0])
    right = q_ref[...].astype(BF16)
    for i in range(last):
        merge_chunk(g_own, f_own, right, merged_ref, term_ref, i)
    for copy in pair:
        copy.wait()
    merge_chunk(g_buf, f_buf, right, merged_ref, term_ref, last)


def whole():
    return pl.BlockSpec(memory_space=pltpu.VMEM)


def in_hbm(count):
    return [pl.BlockSpec(memory_space=pltpu.HBM)] * count


def merge_other(gradient, feedback, right_t):
    half_rows, loaded_rows = pltpu.VMEM((HALF, COLS), BF16), pltpu.VMEM((HALF - CHUNK, COLS), BF16)
    return pl.pallas_call(
        load_kernel,
        in_specs=in_hbm(3),
        out_specs=[whole()] * 5,
        out_shape=[
            half_rows,
            pltpu.VMEM((RANK, HALF), F32),
            loaded_rows,
            loaded_rows,
            pltpu.VMEM((RANK, COLS), F32),
        ],
        scratch_shapes=[
            half_rows,
            half_rows,
            pltpu.SemaphoreType.DMA((2 * CHUNKS - 1,)),
            pltpu.SemaphoreType.DMA((2 * CHUNKS - 1,)),
            pltpu.SemaphoreType.DMA((1,)),
        ],
        compiler_params=pltpu.CompilerParams(vmem_limit_bytes=16 * MIB),
        cost_estimate=pl.CostEstimate(flops=HALF * COLS * RANK * 2, bytes_accessed=8 * HALF * COLS, transcendentals=0),
        name="merge_other",
    )(gradient, feedback, right_t)


def merge_own(gradient, feedback, *loaded):
    return pl.pallas_call(
        merge_kernel,
        in_specs=in_hbm(2) + [whole()] * 3,
        out_specs=[whole(), whole()],
        out_shape=[pltpu.VMEM((HALF, COLS), BF16), pltpu.VMEM((RANK, HALF), F32)],
        scratch_shapes=[
            pltpu.VMEM((HALF, COLS), BF16),
            pltpu.VMEM((HALF, COLS), BF16),
            pltpu.SemaphoreType.DMA((1,)),
            pltpu.SemaphoreType.DMA((1,)),
        ],
        compiler_params=pltpu.CompilerParams(vmem_limit_bytes=16 * MIB),
        cost_estimate=pl.CostEstimate(flops=HALF * COLS * RANK * 2, bytes_accessed=4 * HALF * COLS, transcendentals=0),
        name="merge_own",
    )(gradient, feedback, *loaded)


def right_kernel(merged_ref, left_ref, *refs):
    pair = jnp.concatenate(split(left_ref[...]), axis=0)
    total = jnp.dot(pair, merged_ref[...], preferred_element_type=F32)
    total = total[:RANK] + total[RANK:]
    for ref in refs[:-1]:
        total += ref[...]
    refs[-1][...] = total


def right_term(merged, left, *before):
    return pl.pallas_call(
        right_kernel,
        in_specs=[whole()] * (2 + len(before)),
        out_specs=whole(),
        out_shape=pltpu.VMEM((RANK, COLS), F32),
        compiler_params=pltpu.CompilerParams(vmem_limit_bytes=16 * MIB),
        cost_estimate=pl.CostEstimate(flops=4 * HALF * COLS * RANK, bytes_accessed=2 * HALF * COLS, transcendentals=0),
        name="right_other" if before else "right_own",
    )(merged, left, *before)


def basis_kernel(own_ref, other_ref, inverse_ref, basis_ref):
    own, other = own_ref[...], other_ref[...]
    gram = jnp.zeros((RANK, RANK), F32)
    for part in (own, other):
        gram += lax.dot_general(
            part, part, (((1,), (1,)), ((), ())), precision=lax.Precision.HIGHEST, preferred_element_type=F32
        )
    row = lax.broadcasted_iota(jnp.int32, (RANK, RANK), 0)
    column = lax.broadcasted_iota(jnp.int32, (RANK, RANK), 1)
    eye = jnp.where(row == column, 1.0, 0.0)
    inverse = eye
    for k in range(RANK):
        factor = jnp.where(row[:, :1] > k, gram[:, k : k + 1] / gram[k : k + 1, k : k + 1], 0.0)
        inverse -= factor * inverse[k : k + 1, :]
        gram -= factor * gram[k : k + 1, :]
    pivots = jnp.sum(gram * eye, axis=1, keepdims=True)
    inverse = inverse / jnp.sqrt(pivots)
    inverse_ref[...] = inverse
    for part, start in ((own, 0), (other, HALF)):
        basis = jnp.zeros((RANK, HALF), F32)
        for k in range(RANK):
            basis += inverse[:, k : k + 1] * part[k : k + 1, :]
        high, low = split(basis)
        packed = jnp.concatenate([high, high, low, low], axis=0)
        basis_ref[start : start + HALF, :] = packed.T


def make_basis(own, other):
    return pl.pallas_call(
        basis_kernel,
        in_specs=[whole(), whole()],
        out_specs=[whole(), whole()],
        out_shape=[pltpu.VMEM((RANK, RANK), F32), pltpu.VMEM((ROWS, 4 * RANK), BF16)],
        compiler_params=pltpu.CompilerParams(vmem_limit_bytes=16 * MIB),
        cost_estimate=pl.CostEstimate(flops=4 * ROWS * RANK * RANK, bytes_accessed=4 * MIB, transcendentals=0),
        name="basis",
    )(own, other)


def final_kernel(
    replicas,
    own_ref, other_ref, basis_ref, inverse_ref, sum_ref, near_ref, wrap_ref, far_ref, mom_ref,
    fb_ref, mom_out_ref, right_ref,
    fb_buf, mom_buf, right_buf, fb_sem, mom_sem, right_sem,
):
    total = (sum_ref[...] + near_ref[...]) + (wrap_ref[...] + far_ref[...])
    right = jnp.zeros((RANK, COLS), F32)
    for k in range(RANK):
        right += inverse_ref[:, k : k + 1] * total[k : k + 1, :]
    right = right * (1.0 / replicas)
    right_buf[...] = right
    copies = [pltpu.make_async_copy(right_buf, right_ref, right_sem.at[0])]
    copies[0].start()
    high, low = split(right)
    pack = jnp.concatenate([high, low, high, low], axis=0)
    mine = own_half()
    for i in range(2 * CHUNKS):
        rows = pl.ds(i * CHUNK, CHUNK)
        merged_ref, half = (own_ref, mine) if i < CHUNKS else (other_ref, 1 - mine)
        merged = merged_ref[pl.ds(i % CHUNKS * CHUNK, CHUNK), :]
        approx = jnp.dot(basis_ref[rows, :], pack, preferred_element_type=F32)
        fb_buf[rows, :] = (merged.astype(F32) - approx).astype(BF16)
        target = fb_ref.at[0, rows_of(half, i % CHUNKS), :]
        copies.append(pltpu.make_async_copy(fb_buf.at[rows, :], target, fb_sem.at[i]))
        copies[-1].start()
        if i == 0:
            count = mom_ref.shape[0]
            replica, per_half = lax.axis_index("replica"), HALF // count
            start = jnp.where(replica // per_half == mine, 0, HALF) + lax.rem(replica, per_half) * count
            mom_rows = pl.ds(pl.multiple_of(start, count), count)
            approx = jnp.dot(basis_ref[mom_rows, :], pack, preferred_element_type=F32)
            mom_buf[...] = (0.9 * mom_ref[...].astype(F32) + approx).astype(BF16)
            copies.append(pltpu.make_async_copy(mom_buf, mom_out_ref, mom_sem.at[0]))
            copies[-1].start()
    for copy in copies:
        copy.wait()


def finish(replicas, merged_own, merged_other, basis, inverse, parts, momentum):
    mom_rows = momentum.shape[0]

    def body(*refs):
        final_kernel(replicas, *refs)

    return pl.pallas_call(
        body,
        in_specs=[whole()] * 9,
        out_specs=in_hbm(3),
        out_shape=[
            jax.ShapeDtypeStruct((1, ROWS, COLS), BF16),
            jax.ShapeDtypeStruct((mom_rows, COLS), BF16),
            jax.ShapeDtypeStruct((RANK, COLS), F32),
        ],
        scratch_shapes=[
            pltpu.VMEM((ROWS, COLS), BF16),
            pltpu.VMEM((mom_rows, COLS), BF16),
            pltpu.VMEM((RANK, COLS), F32),
            pltpu.SemaphoreType.DMA((2 * CHUNKS,)),
            pltpu.SemaphoreType.DMA((1,)),
            pltpu.SemaphoreType.DMA((1,)),
        ],
        compiler_params=pltpu.CompilerParams(vmem_limit_bytes=20 * MIB),
        cost_estimate=pl.CostEstimate(flops=2 * ROWS * COLS * 32, bytes_accessed=4 * ROWS * COLS, transcendentals=0),
        name="finish",
    )(merged_own, merged_other, basis, inverse, *parts, momentum)


FLIP = {"n": 1, "w": 3, "f": 2}


def move_pairs(moves, swap):
    pairs = []
    for y, core, z, x in itertools.product(range(4), range(2), range(4), range(4)):
        there = {"y": y, "z": z, "x": x}
        for kind, axis in moves[(core + y + z + x) % 2]:
            there[axis] ^= FLIP[kind]
        to = 2 * there["y"] + (core ^ swap)
        pairs.append((16 * (2 * y + core) + 4 * z + x, 16 * to + 4 * there["z"] + there["x"]))
    return pairs


def move(x, moves, swap):
    return lax.ppermute(x, ("replica", "tensor"), move_pairs(moves, swap))


def ring_sum(x, axes):
    near = move(x, [["n" + a] for a in axes], 1)
    wrap = move(x, [["w" + a] for a in axes], 1)
    return x + near + wrap + move(x, [["f" + a] for a in axes], 0)


def sibling(x):
    return lax.ppermute(x, "replica", [(i, i ^ 1) for i in range(lax.axis_size("replica"))])


def shards(gradient, feedback, momentum, right_init):
    gradient = pltpu.with_memory_space_constraint(gradient, pltpu.HBM)
    feedback = pltpu.with_memory_space_constraint(feedback, pltpu.HBM)
    right_t = pltpu.with_memory_space_constraint(right_init.T, pltpu.HBM)
    momentum = pltpu.with_memory_space_constraint(momentum, pltpu.VMEM)
    merged_other, send, *loaded = merge_other(gradient, feedback, right_t)
    received = sibling(send)
    merged_own, keep = merge_own(gradient, feedback, *loaded)
    own = keep + received
    for axes in ("yx", "xz", "zy"):
        own = ring_sum(own, axes)
    other = sibling(own)
    term = right_term(merged_other, other, right_term(merged_own, own))
    inverse, basis = make_basis(own, other)
    term = term + sibling(term)
    parts = [term, *(move(term, [[kind]] * 2, 1) for kind in ("ny", "wy", "fy"))]
    feedback_out, momentum_out, right_t = finish(
        lax.axis_size("replica"), merged_own, merged_other, basis, inverse, parts, momentum
    )
    return feedback_out, momentum_out, right_t.T


def solution(mesh):
    placed = (
        P("replica", None, "tensor"),
        P("replica", None, "tensor"),
        P("replica", "tensor"),
        P("tensor", None),
    )
    return jax.shard_map(
        shards,
        mesh=mesh,
        in_specs=placed,
        out_specs=(P("replica", None, "tensor"), P("replica", "tensor"), P("tensor", None)),
        check_vma=False,
    )
```

```python
import itertools

import jax
import jax.numpy as jnp
from jax import lax
from jax.experimental import pallas as pl
from jax.experimental.pallas import tpu as pltpu
from jax.sharding import PartitionSpec as P

F32, BF16 = jnp.float32, jnp.bfloat16
ROWS, COLS, RANK = 6144, 384, 8
HALF = ROWS // 2
CHUNKS = 3
CHUNK = HALF // CHUNKS
WRITES = ((0, 256), (256, 768), *((i * CHUNK, CHUNK) for i in range(1, 2 * CHUNKS)))
MIB = 1 << 20


def own_half():
    replica, tensor = lax.axis_index("replica"), lax.axis_index("tensor")
    return lax.rem(replica + replica // 2 + tensor + tensor // 4, 2)


def split(x, count):
    terms = []
    for _ in range(count):
        terms.append(x.astype(BF16))
        x = x - terms[-1].astype(F32)
    return terms


def rows_of(half, chunk):
    return pl.ds(pl.multiple_of(half * HALF + chunk * CHUNK, CHUNK), CHUNK)


def merge_chunk(g_ref, f_ref, right, merged_ref, term_ref, i):
    here = pl.ds(i * CHUNK, CHUNK)
    merged = (g_ref[here, :].astype(F32) + f_ref[here, :].astype(F32)).astype(BF16)
    merged_ref[here, :] = merged
    term_ref[:, here] = lax.dot_general(right, merged, (((1,), (1,)), ((), ())), preferred_element_type=F32)


def load_pair(g_ref, f_ref, half, i, g_to, f_to, g_sem, f_sem):
    here = pl.ds(i * CHUNK, CHUNK)
    pair = (
        pltpu.make_async_copy(g_ref.at[0, rows_of(half, i), :], g_to.at[here, :], g_sem),
        pltpu.make_async_copy(f_ref.at[0, rows_of(half, i), :], f_to.at[here, :], f_sem),
    )
    for copy in pair:
        copy.start()
    return pair


def load_kernel(g_ref, f_ref, q_ref, merged_ref, term_ref, g_own, f_own, q_own, g_buf, f_buf, g_sem, f_sem, q_sem):
    mine = own_half()
    q_copy = pltpu.make_async_copy(q_ref, q_own, q_sem.at[0])
    q_copy.start()
    copies = []
    for half, g_to, f_to in ((1 - mine, g_buf, f_buf), (mine, g_own, f_own)):
        for i in range(CHUNKS):
            n = len(copies)
            copies.append(load_pair(g_ref, f_ref, half, i, g_to, f_to, g_sem.at[n], f_sem.at[n]))
    q_copy.wait()
    right = q_own[...].astype(BF16)
    for i, pair in enumerate(copies):
        for copy in pair:
            copy.wait()
        if i < CHUNKS:
            merge_chunk(g_buf, f_buf, right, merged_ref, term_ref, i)


def merge_kernel(g_ref, f_ref, q_ref, merged_ref, term_ref):
    right = q_ref[...].astype(BF16)
    for i in range(CHUNKS):
        merge_chunk(g_ref, f_ref, right, merged_ref, term_ref, i)


def whole():
    return pl.BlockSpec(memory_space=pltpu.VMEM)


def in_hbm(count):
    return [pl.BlockSpec(memory_space=pltpu.HBM)] * count


def merge_other(gradient, feedback, right_t):
    half_rows = pltpu.VMEM((HALF, COLS), BF16)
    return pl.pallas_call(
        load_kernel,
        in_specs=in_hbm(3),
        out_specs=[whole()] * 5,
        out_shape=[
            half_rows,
            pltpu.VMEM((RANK, HALF), F32),
            half_rows,
            half_rows,
            pltpu.VMEM((RANK, COLS), F32),
        ],
        scratch_shapes=[
            half_rows,
            half_rows,
            pltpu.SemaphoreType.DMA((2 * CHUNKS,)),
            pltpu.SemaphoreType.DMA((2 * CHUNKS,)),
            pltpu.SemaphoreType.DMA((1,)),
        ],
        compiler_params=pltpu.CompilerParams(vmem_limit_bytes=16 * MIB),
        cost_estimate=pl.CostEstimate(flops=HALF * COLS * RANK * 2, bytes_accessed=8 * HALF * COLS, transcendentals=0),
        name="merge_other",
    )(gradient, feedback, right_t)


def merge_own(gradient, feedback, right_t):
    return pl.pallas_call(
        merge_kernel,
        in_specs=[whole()] * 3,
        out_specs=[whole(), whole()],
        out_shape=[pltpu.VMEM((HALF, COLS), BF16), pltpu.VMEM((RANK, HALF), F32)],
        compiler_params=pltpu.CompilerParams(vmem_limit_bytes=16 * MIB),
        cost_estimate=pl.CostEstimate(flops=HALF * COLS * RANK * 2, bytes_accessed=4 * HALF * COLS, transcendentals=0),
        name="merge_own",
    )(gradient, feedback, right_t)


def right_kernel(merged_ref, left_ref, *refs):
    terms = jnp.concatenate(split(left_ref[...], 3), axis=0)
    total = jnp.dot(terms, merged_ref[...], preferred_element_type=F32)
    total = total[2 * RANK :] + total[RANK : 2 * RANK] + total[:RANK]
    for ref in refs[:-1]:
        total += ref[...]
    refs[-1][...] = total


def right_term(merged, left, *before):
    return pl.pallas_call(
        right_kernel,
        in_specs=[whole()] * (2 + len(before)),
        out_specs=whole(),
        out_shape=pltpu.VMEM((RANK, COLS), F32),
        compiler_params=pltpu.CompilerParams(vmem_limit_bytes=16 * MIB),
        cost_estimate=pl.CostEstimate(flops=4 * HALF * COLS * RANK, bytes_accessed=2 * HALF * COLS, transcendentals=0),
        name="right_other" if before else "right_own",
    )(merged, left, *before)


def basis_kernel(own_ref, other_ref, inverse_ref, basis_ref):
    own, other = own_ref[...], other_ref[...]
    gram = jnp.zeros((RANK, RANK), F32)
    for part in (own, other):
        gram += lax.dot_general(
            part, part, (((1,), (1,)), ((), ())), precision=lax.Precision.HIGHEST, preferred_element_type=F32
        )
    row = lax.broadcasted_iota(jnp.int32, (RANK, RANK), 0)
    column = lax.broadcasted_iota(jnp.int32, (RANK, RANK), 1)
    eye = jnp.where(row == column, 1.0, 0.0)
    inverse = eye
    for k in range(RANK):
        factor = jnp.where(row[:, :1] > k, gram[:, k : k + 1] / gram[k : k + 1, k : k + 1], 0.0)
        inverse -= factor * inverse[k : k + 1, :]
        gram -= factor * gram[k : k + 1, :]
    pivots = jnp.sum(gram * eye, axis=1, keepdims=True)
    inverse = inverse / jnp.sqrt(pivots)
    inverse_ref[...] = inverse
    for part, start in ((own, 0), (other, HALF)):
        basis = jnp.zeros((RANK, HALF), F32)
        for k in range(RANK):
            basis += inverse[:, k : k + 1] * part[k : k + 1, :]
        high, low = split(basis, 2)
        packed = jnp.concatenate([high, high, low, low], axis=0)
        basis_ref[start : start + HALF, :] = packed.T


def make_basis(own, other):
    return pl.pallas_call(
        basis_kernel,
        in_specs=[whole(), whole()],
        out_specs=[whole(), whole()],
        out_shape=[pltpu.VMEM((RANK, RANK), F32), pltpu.VMEM((ROWS, 4 * RANK), BF16)],
        compiler_params=pltpu.CompilerParams(vmem_limit_bytes=16 * MIB),
        cost_estimate=pl.CostEstimate(flops=4 * ROWS * RANK * RANK, bytes_accessed=4 * MIB, transcendentals=0),
        name="basis",
    )(own, other)


def final_kernel(
    replicas,
    own_ref, other_ref, basis_ref, inverse_ref, sum_ref, near_ref, wrap_ref, far_ref, mom_ref,
    fb_ref, mom_out_ref, right_ref,
    fb_buf, mom_buf, right_buf, fb_sem, mom_sem, right_sem,
):
    total = (sum_ref[...] + near_ref[...]) + (wrap_ref[...] + far_ref[...])
    right = jnp.zeros((RANK, COLS), F32)
    for k in range(RANK):
        right += inverse_ref[:, k : k + 1] * total[k : k + 1, :]
    right = right * (1.0 / replicas)
    right_buf[...] = right
    copies = [pltpu.make_async_copy(right_buf, right_ref, right_sem.at[0])]
    copies[0].start()
    high, low = split(right, 2)
    pack = jnp.concatenate([high, low, high, low], axis=0)
    mine = own_half()
    for i, (start, count) in enumerate(WRITES):
        rows = pl.ds(start, count)
        merged_ref, half, low_row = (own_ref, mine, start) if start < HALF else (other_ref, 1 - mine, start - HALF)
        merged = merged_ref[pl.ds(low_row, count), :]
        approx = jnp.dot(basis_ref[rows, :], pack, preferred_element_type=F32)
        fb_buf[rows, :] = (merged.astype(F32) - approx).astype(BF16)
        target = fb_ref.at[0, pl.ds(pl.multiple_of(half * HALF + low_row, WRITES[0][1]), count), :]
        copies.append(pltpu.make_async_copy(fb_buf.at[rows, :], target, fb_sem.at[i]))
        copies[-1].start()
        if i == 1:
            count = mom_ref.shape[0]
            replica, per_half = lax.axis_index("replica"), HALF // count
            start = jnp.where(replica // per_half == mine, 0, HALF) + lax.rem(replica, per_half) * count
            mom_rows = pl.ds(pl.multiple_of(start, count), count)
            approx = jnp.dot(basis_ref[mom_rows, :], pack, preferred_element_type=F32)
            mom_buf[...] = (0.9 * mom_ref[...].astype(F32) + approx).astype(BF16)
            copies.append(pltpu.make_async_copy(mom_buf, mom_out_ref, mom_sem.at[0]))
            copies[-1].start()
    for copy in copies:
        copy.wait()


def finish(replicas, merged_own, merged_other, basis, inverse, parts, momentum):
    mom_rows = momentum.shape[0]

    def body(*refs):
        final_kernel(replicas, *refs)

    return pl.pallas_call(
        body,
        in_specs=[whole()] * 9,
        out_specs=in_hbm(3),
        out_shape=[
            jax.ShapeDtypeStruct((1, ROWS, COLS), BF16),
            jax.ShapeDtypeStruct((mom_rows, COLS), BF16),
            jax.ShapeDtypeStruct((RANK, COLS), F32),
        ],
        scratch_shapes=[
            pltpu.VMEM((ROWS, COLS), BF16),
            pltpu.VMEM((mom_rows, COLS), BF16),
            pltpu.VMEM((RANK, COLS), F32),
            pltpu.SemaphoreType.DMA((len(WRITES),)),
            pltpu.SemaphoreType.DMA((1,)),
            pltpu.SemaphoreType.DMA((1,)),
        ],
        compiler_params=pltpu.CompilerParams(vmem_limit_bytes=20 * MIB),
        cost_estimate=pl.CostEstimate(flops=2 * ROWS * COLS * 32, bytes_accessed=4 * ROWS * COLS, transcendentals=0),
        name="finish",
    )(merged_own, merged_other, basis, inverse, *parts, momentum)


FLIP = {"n": 1, "w": 3, "f": 2}


def move_pairs(moves, swap):
    pairs = []
    for y, core, z, x in itertools.product(range(4), range(2), range(4), range(4)):
        there = {"y": y, "z": z, "x": x}
        for kind, axis in moves[(core + y + z + x) % 2]:
            there[axis] ^= FLIP[kind]
        to = 2 * there["y"] + (core ^ swap)
        pairs.append((16 * (2 * y + core) + 4 * z + x, 16 * to + 4 * there["z"] + there["x"]))
    return pairs


def move(x, moves, swap):
    return lax.ppermute(x, ("replica", "tensor"), move_pairs(moves, swap))


def ring_sum(x, axes):
    near = move(x, [["n" + a] for a in axes], 1)
    wrap = move(x, [["w" + a] for a in axes], 1)
    return x + near + wrap + move(x, [["f" + a] for a in axes], 0)


def sibling(x):
    return lax.ppermute(x, "replica", [(i, i ^ 1) for i in range(lax.axis_size("replica"))])


def shards(gradient, feedback, momentum, right_init):
    gradient = pltpu.with_memory_space_constraint(gradient, pltpu.HBM)
    feedback = pltpu.with_memory_space_constraint(feedback, pltpu.HBM)
    right_t = pltpu.with_memory_space_constraint(right_init.T, pltpu.HBM)
    momentum = pltpu.with_memory_space_constraint(momentum, pltpu.VMEM)
    merged_other, send, *loaded = merge_other(gradient, feedback, right_t)
    received = sibling(send)
    merged_own, keep = merge_own(*loaded)
    own = keep + received
    for axes in ("yx", "xz", "zy"):
        own = ring_sum(own, axes)
    other = sibling(own)
    term = right_term(merged_other, other, right_term(merged_own, own))
    inverse, basis = make_basis(own, other)
    term = term + sibling(term)
    parts = [term, *(move(term, [[kind]] * 2, 1) for kind in ("ny", "wy", "fy"))]
    feedback_out, momentum_out, right_t = finish(
        lax.axis_size("replica"), merged_own, merged_other, basis, inverse, parts, momentum
    )
    return feedback_out, momentum_out, right_t.T


def solution(mesh):
    placed = (
        P("replica", None, "tensor"),
        P("replica", None, "tensor"),
        P("replica", "tensor"),
        P("tensor", None),
    )
    return jax.shard_map(
        shards,
        mesh=mesh,
        in_specs=placed,
        out_specs=(P("replica", None, "tensor"), P("replica", "tensor"), P("tensor", None)),
        check_vma=False,
    )
```

```python
import jax
import jax.numpy as jnp
from jax import lax
from jax.experimental import pallas as pl
from jax.experimental.pallas import tpu as pltpu
from jax.sharding import PartitionSpec as P

F32, BF16 = jnp.float32, jnp.bfloat16
ROWS, COLS, RANK = 6144, 384, 8
HALF = ROWS // 2
CHUNKS = 3
CHUNK = HALF // CHUNKS
WRITES = [(i * CHUNK, CHUNK) for i in range(2 * CHUNKS)]
MIB = 1 << 20


def own_half():
    replica, tensor = lax.axis_index("replica"), lax.axis_index("tensor")
    bits = replica + replica // 2 + replica // 4 + tensor + tensor // 2 + tensor // 4 + tensor // 8
    return lax.rem(bits, 2)


def split(x, count):
    terms = []
    for _ in range(count):
        terms.append(x.astype(BF16))
        x = x - terms[-1].astype(F32)
    return terms


def rows_of(half, chunk):
    return pl.ds(pl.multiple_of(half * HALF + chunk * CHUNK, CHUNK), CHUNK)


def merge_chunk(g_ref, f_ref, right, merged_ref, term_ref, i):
    here = pl.ds(i * CHUNK, CHUNK)
    merged = (g_ref[here, :].astype(F32) + f_ref[here, :].astype(F32)).astype(BF16)
    merged_ref[here, :] = merged
    term_ref[:, here] = lax.dot_general(right, merged, (((1,), (1,)), ((), ())), preferred_element_type=F32)


def load_pair(g_ref, f_ref, half, i, g_to, f_to, g_sem, f_sem):
    here = pl.ds(i * CHUNK, CHUNK)
    pair = (
        pltpu.make_async_copy(g_ref.at[0, rows_of(half, i), :], g_to.at[here, :], g_sem),
        pltpu.make_async_copy(f_ref.at[0, rows_of(half, i), :], f_to.at[here, :], f_sem),
    )
    for copy in pair:
        copy.start()
    return pair


def load_kernel(g_ref, f_ref, q_ref, merged_ref, term_ref, g_own, f_own, q_own, g_buf, f_buf, g_sem, f_sem, q_sem):
    mine = own_half()
    q_copy = pltpu.make_async_copy(q_ref, q_own, q_sem.at[0])
    q_copy.start()
    copies = []
    for half, g_to, f_to in ((1 - mine, g_buf, f_buf), (mine, g_own, f_own)):
        for i in range(CHUNKS):
            n = len(copies)
            copies.append(load_pair(g_ref, f_ref, half, i, g_to, f_to, g_sem.at[n], f_sem.at[n]))
    q_copy.wait()
    right = q_own[...].astype(BF16)
    for i, pair in enumerate(copies):
        for copy in pair:
            copy.wait()
        if i < CHUNKS:
            merge_chunk(g_buf, f_buf, right, merged_ref, term_ref, i)


def merge_kernel(g_ref, f_ref, q_ref, merged_ref, term_ref):
    right = q_ref[...].astype(BF16)
    for i in range(CHUNKS):
        merge_chunk(g_ref, f_ref, right, merged_ref, term_ref, i)


def whole():
    return pl.BlockSpec(memory_space=pltpu.VMEM)


def in_hbm(count):
    return [pl.BlockSpec(memory_space=pltpu.HBM)] * count


def merge_other(gradient, feedback, right_t):
    half_rows = pltpu.VMEM((HALF, COLS), BF16)
    return pl.pallas_call(
        load_kernel,
        in_specs=in_hbm(3),
        out_specs=[whole()] * 5,
        out_shape=[
            half_rows,
            pltpu.VMEM((RANK, HALF), F32),
            half_rows,
            half_rows,
            pltpu.VMEM((RANK, COLS), F32),
        ],
        scratch_shapes=[
            half_rows,
            half_rows,
            pltpu.SemaphoreType.DMA((2 * CHUNKS,)),
            pltpu.SemaphoreType.DMA((2 * CHUNKS,)),
            pltpu.SemaphoreType.DMA((1,)),
        ],
        compiler_params=pltpu.CompilerParams(vmem_limit_bytes=16 * MIB),
        cost_estimate=pl.CostEstimate(flops=HALF * COLS * RANK * 2, bytes_accessed=8 * HALF * COLS, transcendentals=0),
        name="merge_other",
    )(gradient, feedback, right_t)


def merge_own(gradient, feedback, right_t):
    return pl.pallas_call(
        merge_kernel,
        in_specs=[whole()] * 3,
        out_specs=[whole(), whole()],
        out_shape=[pltpu.VMEM((HALF, COLS), BF16), pltpu.VMEM((RANK, HALF), F32)],
        compiler_params=pltpu.CompilerParams(vmem_limit_bytes=16 * MIB),
        cost_estimate=pl.CostEstimate(flops=HALF * COLS * RANK * 2, bytes_accessed=4 * HALF * COLS, transcendentals=0),
        name="merge_own",
    )(gradient, feedback, right_t)


def right_kernel(merged_ref, left_ref, *refs):
    terms = jnp.concatenate(split(left_ref[...], 3), axis=0)
    total = jnp.dot(terms, merged_ref[...], preferred_element_type=F32)
    total = total[2 * RANK :] + total[RANK : 2 * RANK] + total[:RANK]
    for ref in refs[:-1]:
        total += ref[...]
    refs[-1][...] = total


def right_term(merged, left, *before):
    return pl.pallas_call(
        right_kernel,
        in_specs=[whole()] * (2 + len(before)),
        out_specs=whole(),
        out_shape=pltpu.VMEM((RANK, COLS), F32),
        compiler_params=pltpu.CompilerParams(vmem_limit_bytes=16 * MIB),
        cost_estimate=pl.CostEstimate(flops=4 * HALF * COLS * RANK, bytes_accessed=2 * HALF * COLS, transcendentals=0),
        name="right_other" if before else "right_own",
    )(merged, left, *before)


def basis_kernel(own_ref, other_ref, inverse_ref, basis_ref):
    own, other = own_ref[...], other_ref[...]
    gram = jnp.zeros((RANK, RANK), F32)
    for part in (own, other):
        gram += lax.dot_general(
            part, part, (((1,), (1,)), ((), ())), precision=lax.Precision.HIGHEST, preferred_element_type=F32
        )
    row = lax.broadcasted_iota(jnp.int32, (RANK, RANK), 0)
    column = lax.broadcasted_iota(jnp.int32, (RANK, RANK), 1)
    eye = jnp.where(row == column, 1.0, 0.0)
    inverse = eye
    for k in range(RANK):
        factor = jnp.where(row[:, :1] > k, gram[:, k : k + 1] / gram[k : k + 1, k : k + 1], 0.0)
        inverse -= factor * inverse[k : k + 1, :]
        gram -= factor * gram[k : k + 1, :]
    pivots = jnp.sum(gram * eye, axis=1, keepdims=True)
    inverse = inverse / jnp.sqrt(pivots)
    inverse_ref[...] = inverse
    for part, start in ((own, 0), (other, HALF)):
        basis = jnp.zeros((RANK, HALF), F32)
        for k in range(RANK):
            basis += inverse[:, k : k + 1] * part[k : k + 1, :]
        high, low = split(basis, 2)
        packed = jnp.concatenate([high, high, low, low], axis=0)
        basis_ref[start : start + HALF, :] = packed.T


def make_basis(own, other):
    return pl.pallas_call(
        basis_kernel,
        in_specs=[whole(), whole()],
        out_specs=[whole(), whole()],
        out_shape=[pltpu.VMEM((RANK, RANK), F32), pltpu.VMEM((ROWS, 4 * RANK), BF16)],
        compiler_params=pltpu.CompilerParams(vmem_limit_bytes=16 * MIB),
        cost_estimate=pl.CostEstimate(flops=4 * ROWS * RANK * RANK, bytes_accessed=4 * MIB, transcendentals=0),
        name="basis",
    )(own, other)


def final_kernel(
    replicas,
    own_ref, other_ref, basis_ref, inverse_ref, sum_ref, near_ref, wrap_ref, far_ref, mom_ref,
    fb_ref, mom_out_ref, right_ref,
    fb_buf, mom_buf, right_buf, fb_sem, mom_sem, right_sem,
):
    total = (sum_ref[...] + near_ref[...]) + (wrap_ref[...] + far_ref[...])
    right = jnp.zeros((RANK, COLS), F32)
    for k in range(RANK):
        right += inverse_ref[:, k : k + 1] * total[k : k + 1, :]
    right = right * (1.0 / replicas)
    right_buf[...] = right
    copies = [pltpu.make_async_copy(right_buf, right_ref, right_sem.at[0])]
    copies[0].start()
    high, low = split(right, 2)
    pack = jnp.concatenate([high, low, high, low], axis=0)
    mine = own_half()
    for i, (start, count) in enumerate(WRITES):
        rows = pl.ds(start, count)
        merged_ref, half, low_row = (own_ref, mine, start) if start < HALF else (other_ref, 1 - mine, start - HALF)
        merged = merged_ref[pl.ds(low_row, count), :]
        approx = jnp.dot(basis_ref[rows, :], pack, preferred_element_type=F32)
        fb_buf[rows, :] = (merged.astype(F32) - approx).astype(BF16)
        target = fb_ref.at[0, pl.ds(pl.multiple_of(half * HALF + low_row, WRITES[0][1]), count), :]
        copies.append(pltpu.make_async_copy(fb_buf.at[rows, :], target, fb_sem.at[i]))
        copies[-1].start()
        if i == 0:
            count = mom_ref.shape[0]
            replica, per_half = lax.axis_index("replica"), HALF // count
            start = jnp.where(replica // per_half == mine, 0, HALF) + lax.rem(replica, per_half) * count
            mom_rows = pl.ds(pl.multiple_of(start, count), count)
            approx = jnp.dot(basis_ref[mom_rows, :], pack, preferred_element_type=F32)
            mom_buf[...] = (0.9 * mom_ref[...].astype(F32) + approx).astype(BF16)
            copies.append(pltpu.make_async_copy(mom_buf, mom_out_ref, mom_sem.at[0]))
            copies[-1].start()
    for copy in copies:
        copy.wait()


def finish(replicas, merged_own, merged_other, basis, inverse, parts, momentum):
    mom_rows = momentum.shape[0]

    def body(*refs):
        final_kernel(replicas, *refs)

    return pl.pallas_call(
        body,
        in_specs=[whole()] * 9,
        out_specs=in_hbm(3),
        out_shape=[
            jax.ShapeDtypeStruct((1, ROWS, COLS), BF16),
            jax.ShapeDtypeStruct((mom_rows, COLS), BF16),
            jax.ShapeDtypeStruct((RANK, COLS), F32),
        ],
        scratch_shapes=[
            pltpu.VMEM((ROWS, COLS), BF16),
            pltpu.VMEM((mom_rows, COLS), BF16),
            pltpu.VMEM((RANK, COLS), F32),
            pltpu.SemaphoreType.DMA((len(WRITES),)),
            pltpu.SemaphoreType.DMA((1,)),
            pltpu.SemaphoreType.DMA((1,)),
        ],
        compiler_params=pltpu.CompilerParams(vmem_limit_bytes=20 * MIB),
        cost_estimate=pl.CostEstimate(flops=2 * ROWS * COLS * 32, bytes_accessed=4 * ROWS * COLS, transcendentals=0),
        name="finish",
    )(merged_own, merged_other, basis, inverse, *parts, momentum)


CORE, LOW = 16, {"y": 32, "z": 4, "x": 1}


def swap(x, masks):
    pairs = [(i, i ^ masks[i.bit_count() % 2]) for i in range(128)]
    return lax.ppermute(x, ("replica", "tensor"), pairs)


def ring_sum(x, axes):
    near = swap(x, [LOW[a] | CORE for a in axes])
    wrap = swap(x, [3 * LOW[a] for a in axes])
    return x + near + wrap + swap(x, [2 * LOW[a] | CORE for a in axes])


def sibling(x):
    return swap(x, [CORE] * 2)


def shards(gradient, feedback, momentum, right_init):
    gradient = pltpu.with_memory_space_constraint(gradient, pltpu.HBM)
    feedback = pltpu.with_memory_space_constraint(feedback, pltpu.HBM)
    right_t = pltpu.with_memory_space_constraint(right_init.T, pltpu.HBM)
    momentum = pltpu.with_memory_space_constraint(momentum, pltpu.VMEM)
    merged_other, send, *loaded = merge_other(gradient, feedback, right_t)
    received = sibling(send)
    merged_own, keep = merge_own(*loaded)
    own = keep + received
    for axes in ("yx", "xz", "zy"):
        own = ring_sum(own, axes)
    other = sibling(own)
    term = right_term(merged_other, other, right_term(merged_own, own))
    inverse, basis = make_basis(own, other)
    term = term + sibling(term)
    parts = [term, *(swap(term, [steps * LOW["y"] | CORE] * 2) for steps in (1, 3, 2))]
    feedback_out, momentum_out, right_t = finish(
        lax.axis_size("replica"), merged_own, merged_other, basis, inverse, parts, momentum
    )
    return feedback_out, momentum_out, right_t.T


def solution(mesh):
    placed = (
        P("replica", None, "tensor"),
        P("replica", None, "tensor"),
        P("replica", "tensor"),
        P("tensor", None),
    )
    return jax.shard_map(
        shards,
        mesh=mesh,
        in_specs=placed,
        out_specs=(P("replica", None, "tensor"), P("replica", "tensor"), P("tensor", None)),
        check_vma=False,
    )
```

```python
import jax
import jax.numpy as jnp
from jax import lax
from jax.experimental import pallas as pl
from jax.experimental.pallas import tpu as pltpu
from jax.sharding import PartitionSpec as P

F32, BF16 = jnp.float32, jnp.bfloat16
ROWS, COLS, RANK = 6144, 384, 8
HALF = ROWS // 2
CHUNKS = 3
CHUNK = HALF // CHUNKS
WRITES = [(i * CHUNK, CHUNK) for i in range(2 * CHUNKS)]
LANES = 128
MIB = 1 << 20


def own_half():
    replica, tensor = lax.axis_index("replica"), lax.axis_index("tensor")
    bits = replica + replica // 2 + replica // 4 + tensor + tensor // 2 + tensor // 4 + tensor // 8
    return lax.rem(bits, 2)


def split(x, count):
    terms = []
    for _ in range(count):
        terms.append(x.astype(BF16))
        x = x - terms[-1].astype(F32)
    return terms


def rows_of(half, chunk):
    return pl.ds(pl.multiple_of(half * HALF + chunk * CHUNK, CHUNK), CHUNK)


def merge_chunk(g_ref, f_ref, right, merged_ref, term_ref, i):
    here = pl.ds(i * CHUNK, CHUNK)
    merged = (g_ref[here, :].astype(F32) + f_ref[here, :].astype(F32)).astype(BF16)
    merged_ref[here, :] = merged
    term_ref[:, here] = lax.dot_general(right, merged, (((1,), (1,)), ((), ())), preferred_element_type=F32)


def load_pair(g_ref, f_ref, half, i, g_to, f_to, g_sem, f_sem):
    here = pl.ds(i * CHUNK, CHUNK)
    pair = (
        pltpu.make_async_copy(g_ref.at[0, rows_of(half, i), :], g_to.at[here, :], g_sem),
        pltpu.make_async_copy(f_ref.at[0, rows_of(half, i), :], f_to.at[here, :], f_sem),
    )
    for copy in pair:
        copy.start()
    return pair


def load_kernel(g_ref, f_ref, q_ref, merged_ref, term_ref, g_own, f_own, q_own, g_buf, f_buf, g_sem, f_sem, q_sem):
    mine = own_half()
    q_copy = pltpu.make_async_copy(q_ref, q_own, q_sem.at[0])
    q_copy.start()
    copies = []
    for half, g_to, f_to in ((1 - mine, g_buf, f_buf), (mine, g_own, f_own)):
        for i in range(CHUNKS):
            n = len(copies)
            copies.append(load_pair(g_ref, f_ref, half, i, g_to, f_to, g_sem.at[n], f_sem.at[n]))
    q_copy.wait()
    right = q_own[...].astype(BF16)
    for i, pair in enumerate(copies):
        for copy in pair:
            copy.wait()
        if i < CHUNKS:
            merge_chunk(g_buf, f_buf, right, merged_ref, term_ref, i)


def merge_kernel(g_ref, f_ref, q_ref, merged_ref, term_ref):
    right = q_ref[...].astype(BF16)
    for i in range(CHUNKS):
        merge_chunk(g_ref, f_ref, right, merged_ref, term_ref, i)


def whole():
    return pl.BlockSpec(memory_space=pltpu.VMEM)


def in_hbm(count):
    return [pl.BlockSpec(memory_space=pltpu.HBM)] * count


def merge_other(gradient, feedback, right_t):
    half_rows = pltpu.VMEM((HALF, COLS), BF16)
    return pl.pallas_call(
        load_kernel,
        in_specs=in_hbm(3),
        out_specs=[whole()] * 5,
        out_shape=[
            half_rows,
            pltpu.VMEM((RANK, HALF), F32),
            half_rows,
            half_rows,
            pltpu.VMEM((RANK, COLS), F32),
        ],
        scratch_shapes=[
            half_rows,
            half_rows,
            pltpu.SemaphoreType.DMA((2 * CHUNKS,)),
            pltpu.SemaphoreType.DMA((2 * CHUNKS,)),
            pltpu.SemaphoreType.DMA((1,)),
        ],
        compiler_params=pltpu.CompilerParams(vmem_limit_bytes=16 * MIB),
        cost_estimate=pl.CostEstimate(flops=HALF * COLS * RANK * 2, bytes_accessed=8 * HALF * COLS, transcendentals=0),
        name="merge_other",
    )(gradient, feedback, right_t)


def merge_own(gradient, feedback, right_t):
    return pl.pallas_call(
        merge_kernel,
        in_specs=[whole()] * 3,
        out_specs=[whole(), whole()],
        out_shape=[pltpu.VMEM((HALF, COLS), BF16), pltpu.VMEM((RANK, HALF), F32)],
        compiler_params=pltpu.CompilerParams(vmem_limit_bytes=16 * MIB),
        cost_estimate=pl.CostEstimate(flops=HALF * COLS * RANK * 2, bytes_accessed=4 * HALF * COLS, transcendentals=0),
        name="merge_own",
    )(gradient, feedback, right_t)


def right_kernel(merged_ref, left_ref, *refs):
    terms = jnp.concatenate(split(left_ref[...], 3), axis=0)
    total = jnp.dot(terms, merged_ref[...], preferred_element_type=F32)
    total = total[2 * RANK :] + total[RANK : 2 * RANK] + total[:RANK]
    for ref in refs[:-1]:
        total += ref[...]
    refs[-1][...] = total


def right_term(merged, left, *before):
    return pl.pallas_call(
        right_kernel,
        in_specs=[whole()] * (2 + len(before)),
        out_specs=whole(),
        out_shape=pltpu.VMEM((RANK, COLS), F32),
        compiler_params=pltpu.CompilerParams(vmem_limit_bytes=16 * MIB),
        cost_estimate=pl.CostEstimate(flops=4 * HALF * COLS * RANK, bytes_accessed=2 * HALF * COLS, transcendentals=0),
        name="right_other" if before else "right_own",
    )(merged, left, *before)


def basis_kernel(replicas, own_ref, other_ref, inverse_ref, basis_ref):
    own, other = own_ref[...], other_ref[...]
    gram = jnp.zeros((RANK, RANK), F32)
    for part in (own, other):
        gram += lax.dot_general(
            part, part, (((1,), (1,)), ((), ())), precision=lax.Precision.HIGHEST, preferred_element_type=F32
        )
    row = lax.broadcasted_iota(jnp.int32, (RANK, RANK), 0)
    column = lax.broadcasted_iota(jnp.int32, (RANK, RANK), 1)
    eye = jnp.where(row == column, 1.0, 0.0)
    inverse = eye
    for k in range(RANK):
        factor = jnp.where(row[:, :1] > k, gram[:, k : k + 1] / gram[k : k + 1, k : k + 1], 0.0)
        inverse -= factor * inverse[k : k + 1, :]
        gram -= factor * gram[k : k + 1, :]
    pivots = jnp.sum(gram * eye, axis=1, keepdims=True)
    inverse = inverse / jnp.sqrt(pivots)
    for k in range(RANK):
        column = inverse[:, k : k + 1] * (1.0 / replicas)
        inverse_ref[k * RANK : (k + 1) * RANK, :] = jnp.broadcast_to(column, (RANK, LANES))
    for part, start in ((own, 0), (other, HALF)):
        basis = jnp.zeros((RANK, HALF), F32)
        for k in range(RANK):
            basis += inverse[:, k : k + 1] * part[k : k + 1, :]
        high, low = split(basis, 2)
        packed = jnp.concatenate([high, high, low, low], axis=0)
        basis_ref[start : start + HALF, :] = packed.T


def make_basis(replicas, own, other):
    def body(*refs):
        basis_kernel(replicas, *refs)

    return pl.pallas_call(
        body,
        in_specs=[whole(), whole()],
        out_specs=[whole(), whole()],
        out_shape=[pltpu.VMEM((RANK * RANK, LANES), F32), pltpu.VMEM((ROWS, 4 * RANK), BF16)],
        compiler_params=pltpu.CompilerParams(vmem_limit_bytes=16 * MIB),
        cost_estimate=pl.CostEstimate(flops=4 * ROWS * RANK * RANK, bytes_accessed=4 * MIB, transcendentals=0),
        name="basis",
    )(own, other)


def final_kernel(
    own_ref, other_ref, basis_ref, inverse_ref, sum_ref, near_ref, wrap_ref, far_ref, mom_ref,
    fb_ref, mom_out_ref, right_ref,
    fb_buf, mom_buf, right_buf, fb_sem, mom_sem, right_sem,
):
    total = (sum_ref[...] + near_ref[...]) + (wrap_ref[...] + far_ref[...])
    pieces = []
    for start in range(0, COLS, LANES):
        piece = jnp.zeros((RANK, LANES), F32)
        for k in range(RANK):
            piece += inverse_ref[k * RANK : (k + 1) * RANK, :] * total[k : k + 1, start : start + LANES]
        pieces.append(piece)
    right = jnp.concatenate(pieces, axis=1)
    right_buf[...] = right
    copies = [pltpu.make_async_copy(right_buf, right_ref, right_sem.at[0])]
    copies[0].start()
    high, low = split(right, 2)
    pack = jnp.concatenate([high, low, high, low], axis=0)
    mine = own_half()
    for i, (start, count) in enumerate(WRITES):
        rows = pl.ds(start, count)
        merged_ref, half, low_row = (own_ref, mine, start) if start < HALF else (other_ref, 1 - mine, start - HALF)
        merged = merged_ref[pl.ds(low_row, count), :]
        approx = jnp.dot(basis_ref[rows, :], pack, preferred_element_type=F32)
        fb_buf[rows, :] = (merged.astype(F32) - approx).astype(BF16)
        target = fb_ref.at[0, pl.ds(pl.multiple_of(half * HALF + low_row, WRITES[0][1]), count), :]
        copies.append(pltpu.make_async_copy(fb_buf.at[rows, :], target, fb_sem.at[i]))
        copies[-1].start()
        if i == 0:
            count = mom_ref.shape[0]
            replica, per_half = lax.axis_index("replica"), HALF // count
            start = jnp.where(replica // per_half == mine, 0, HALF) + lax.rem(replica, per_half) * count
            mom_rows = pl.ds(pl.multiple_of(start, count), count)
            approx = jnp.dot(basis_ref[mom_rows, :], pack, preferred_element_type=F32)
            mom_buf[...] = (0.9 * mom_ref[...].astype(F32) + approx).astype(BF16)
            copies.append(pltpu.make_async_copy(mom_buf, mom_out_ref, mom_sem.at[0]))
            copies[-1].start()
    for copy in copies:
        copy.wait()


def finish(merged_own, merged_other, basis, inverse, parts, momentum):
    mom_rows = momentum.shape[0]
    return pl.pallas_call(
        final_kernel,
        in_specs=[whole()] * 9,
        out_specs=in_hbm(3),
        out_shape=[
            jax.ShapeDtypeStruct((1, ROWS, COLS), BF16),
            jax.ShapeDtypeStruct((mom_rows, COLS), BF16),
            jax.ShapeDtypeStruct((RANK, COLS), F32),
        ],
        scratch_shapes=[
            pltpu.VMEM((ROWS, COLS), BF16),
            pltpu.VMEM((mom_rows, COLS), BF16),
            pltpu.VMEM((RANK, COLS), F32),
            pltpu.SemaphoreType.DMA((len(WRITES),)),
            pltpu.SemaphoreType.DMA((1,)),
            pltpu.SemaphoreType.DMA((1,)),
        ],
        compiler_params=pltpu.CompilerParams(vmem_limit_bytes=20 * MIB),
        cost_estimate=pl.CostEstimate(flops=2 * ROWS * COLS * 32, bytes_accessed=4 * ROWS * COLS, transcendentals=0),
        name="finish",
    )(merged_own, merged_other, basis, inverse, *parts, momentum)


CORE, LOW = 16, {"y": 32, "z": 4, "x": 1}


def swap(x, masks):
    pairs = [(i, i ^ masks[i.bit_count() % 2]) for i in range(128)]
    return lax.ppermute(x, ("replica", "tensor"), pairs)


def ring_sum(x, axes):
    near = swap(x, [LOW[a] | CORE for a in axes])
    wrap = swap(x, [3 * LOW[a] for a in axes])
    return x + near + wrap + swap(x, [2 * LOW[a] | CORE for a in axes])


def sibling(x):
    return swap(x, [CORE] * 2)


def shards(gradient, feedback, momentum, right_init):
    gradient = pltpu.with_memory_space_constraint(gradient, pltpu.HBM)
    feedback = pltpu.with_memory_space_constraint(feedback, pltpu.HBM)
    right_t = pltpu.with_memory_space_constraint(right_init.T, pltpu.HBM)
    momentum = pltpu.with_memory_space_constraint(momentum, pltpu.VMEM)
    merged_other, send, *loaded = merge_other(gradient, feedback, right_t)
    received = sibling(send)
    merged_own, keep = merge_own(*loaded)
    own = keep + received
    for axes in ("yx", "xz", "zy"):
        own = ring_sum(own, axes)
    other = sibling(own)
    term = right_term(merged_other, other, right_term(merged_own, own))
    inverse, basis = make_basis(lax.axis_size("replica"), own, other)
    term = term + sibling(term)
    parts = [term, *(swap(term, [steps * LOW["y"] | CORE] * 2) for steps in (1, 3, 2))]
    feedback_out, momentum_out, right_t = finish(merged_own, merged_other, basis, inverse, parts, momentum)
    return feedback_out, momentum_out, right_t.T


def solution(mesh):
    placed = (
        P("replica", None, "tensor"),
        P("replica", None, "tensor"),
        P("replica", "tensor"),
        P("tensor", None),
    )
    return jax.shard_map(
        shards,
        mesh=mesh,
        in_specs=placed,
        out_specs=(P("replica", None, "tensor"), P("replica", "tensor"), P("tensor", None)),
        check_vma=False,
    )
```

```python
import jax
import jax.numpy as jnp
from jax import lax
from jax.experimental import pallas as pl
from jax.experimental.pallas import tpu as pltpu
from jax.sharding import PartitionSpec as P

F32, BF16 = jnp.float32, jnp.bfloat16
ROWS, COLS, RANK = 6144, 384, 8
HALF = ROWS // 2
CHUNKS = 3
CHUNK = HALF // CHUNKS
WRITES = [(start, HALF // 4) for start in range(0, ROWS, HALF // 4)]
LANES = 128
MIB = 1 << 20


def own_half():
    replica, tensor = lax.axis_index("replica"), lax.axis_index("tensor")
    bits = replica + replica // 2 + replica // 4 + tensor + tensor // 2 + tensor // 4 + tensor // 8
    return lax.rem(bits, 2)


def split(x, count):
    terms = []
    for _ in range(count):
        terms.append(x.astype(BF16))
        x = x - terms[-1].astype(F32)
    return terms


def rows_of(half, chunk):
    return pl.ds(pl.multiple_of(half * HALF + chunk * CHUNK, CHUNK), CHUNK)


def merge_chunk(g_ref, f_ref, right, merged_ref, term_ref, i):
    here = pl.ds(i * CHUNK, CHUNK)
    merged = (g_ref[here, :].astype(F32) + f_ref[here, :].astype(F32)).astype(BF16)
    merged_ref[here, :] = merged
    term_ref[:, here] = lax.dot_general(right, merged, (((1,), (1,)), ((), ())), preferred_element_type=F32)


def load_pair(g_ref, f_ref, half, i, g_to, f_to, g_sem, f_sem):
    here = pl.ds(i * CHUNK, CHUNK)
    pair = (
        pltpu.make_async_copy(g_ref.at[0, rows_of(half, i), :], g_to.at[here, :], g_sem),
        pltpu.make_async_copy(f_ref.at[0, rows_of(half, i), :], f_to.at[here, :], f_sem),
    )
    for copy in pair:
        copy.start()
    return pair


def load_kernel(g_ref, f_ref, q_ref, merged_ref, term_ref, g_own, f_own, q_own, g_buf, f_buf, g_sem, f_sem, q_sem):
    mine = own_half()
    q_copy = pltpu.make_async_copy(q_ref, q_own, q_sem.at[0])
    q_copy.start()
    copies = []
    for half, g_to, f_to in ((1 - mine, g_buf, f_buf), (mine, g_own, f_own)):
        for i in range(CHUNKS):
            n = len(copies)
            copies.append(load_pair(g_ref, f_ref, half, i, g_to, f_to, g_sem.at[n], f_sem.at[n]))
    q_copy.wait()
    right = q_own[...].astype(BF16)
    for i, pair in enumerate(copies):
        for copy in pair:
            copy.wait()
        if i < CHUNKS:
            merge_chunk(g_buf, f_buf, right, merged_ref, term_ref, i)


def merge_kernel(g_ref, f_ref, q_ref, merged_ref, term_ref):
    right = q_ref[...].astype(BF16)
    for i in range(CHUNKS):
        merge_chunk(g_ref, f_ref, right, merged_ref, term_ref, i)


def whole():
    return pl.BlockSpec(memory_space=pltpu.VMEM)


def in_hbm(count):
    return [pl.BlockSpec(memory_space=pltpu.HBM)] * count


def merge_other(gradient, feedback, right_t):
    half_rows = pltpu.VMEM((HALF, COLS), BF16)
    return pl.pallas_call(
        load_kernel,
        in_specs=in_hbm(3),
        out_specs=[whole()] * 5,
        out_shape=[
            half_rows,
            pltpu.VMEM((RANK, HALF), F32),
            half_rows,
            half_rows,
            pltpu.VMEM((RANK, COLS), F32),
        ],
        scratch_shapes=[
            half_rows,
            half_rows,
            pltpu.SemaphoreType.DMA((2 * CHUNKS,)),
            pltpu.SemaphoreType.DMA((2 * CHUNKS,)),
            pltpu.SemaphoreType.DMA((1,)),
        ],
        compiler_params=pltpu.CompilerParams(vmem_limit_bytes=16 * MIB),
        cost_estimate=pl.CostEstimate(flops=HALF * COLS * RANK * 2, bytes_accessed=8 * HALF * COLS, transcendentals=0),
        name="merge_other",
    )(gradient, feedback, right_t)


def merge_own(gradient, feedback, right_t):
    return pl.pallas_call(
        merge_kernel,
        in_specs=[whole()] * 3,
        out_specs=[whole(), whole()],
        out_shape=[pltpu.VMEM((HALF, COLS), BF16), pltpu.VMEM((RANK, HALF), F32)],
        compiler_params=pltpu.CompilerParams(vmem_limit_bytes=16 * MIB),
        cost_estimate=pl.CostEstimate(flops=HALF * COLS * RANK * 2, bytes_accessed=4 * HALF * COLS, transcendentals=0),
        name="merge_own",
    )(gradient, feedback, right_t)


def right_kernel(merged_ref, left_ref, *refs):
    terms = jnp.concatenate(split(left_ref[...], 3), axis=0)
    total = jnp.dot(terms, merged_ref[...], preferred_element_type=F32)
    total = total[2 * RANK :] + total[RANK : 2 * RANK] + total[:RANK]
    for ref in refs[:-1]:
        total += ref[...]
    refs[-1][...] = total


def right_term(merged, left, *before):
    return pl.pallas_call(
        right_kernel,
        in_specs=[whole()] * (2 + len(before)),
        out_specs=whole(),
        out_shape=pltpu.VMEM((RANK, COLS), F32),
        compiler_params=pltpu.CompilerParams(vmem_limit_bytes=16 * MIB),
        cost_estimate=pl.CostEstimate(flops=4 * HALF * COLS * RANK, bytes_accessed=2 * HALF * COLS, transcendentals=0),
        name="right_other" if before else "right_own",
    )(merged, left, *before)


def basis_kernel(replicas, own_ref, other_ref, inverse_ref, basis_ref):
    own, other = own_ref[...], other_ref[...]
    gram = jnp.zeros((RANK, RANK), F32)
    for part in (own, other):
        gram += lax.dot_general(
            part, part, (((1,), (1,)), ((), ())), precision=lax.Precision.HIGHEST, preferred_element_type=F32
        )
    row = lax.broadcasted_iota(jnp.int32, (RANK, RANK), 0)
    column = lax.broadcasted_iota(jnp.int32, (RANK, RANK), 1)
    eye = jnp.where(row == column, 1.0, 0.0)
    inverse = eye
    for k in range(RANK):
        factor = jnp.where(row[:, :1] > k, gram[:, k : k + 1] / gram[k : k + 1, k : k + 1], 0.0)
        inverse -= factor * inverse[k : k + 1, :]
        gram -= factor * gram[k : k + 1, :]
    pivots = jnp.sum(gram * eye, axis=1, keepdims=True)
    inverse = inverse / jnp.sqrt(pivots)
    for k in range(RANK):
        column = inverse[:, k : k + 1] * (1.0 / replicas)
        inverse_ref[k * RANK : (k + 1) * RANK, :] = jnp.broadcast_to(column, (RANK, LANES))
    for part, start in ((own, 0), (other, HALF)):
        basis = jnp.zeros((RANK, HALF), F32)
        for k in range(RANK):
            basis += inverse[:, k : k + 1] * part[k : k + 1, :]
        high, low = split(basis, 2)
        packed = jnp.concatenate([high, high, low, low], axis=0)
        basis_ref[start : start + HALF, :] = packed.T


def make_basis(replicas, own, other):
    def body(*refs):
        basis_kernel(replicas, *refs)

    return pl.pallas_call(
        body,
        in_specs=[whole(), whole()],
        out_specs=[whole(), whole()],
        out_shape=[pltpu.VMEM((RANK * RANK, LANES), F32), pltpu.VMEM((ROWS, 4 * RANK), BF16)],
        compiler_params=pltpu.CompilerParams(vmem_limit_bytes=16 * MIB),
        cost_estimate=pl.CostEstimate(flops=4 * ROWS * RANK * RANK, bytes_accessed=4 * MIB, transcendentals=0),
        name="basis",
    )(own, other)


def final_kernel(
    own_ref, other_ref, basis_ref, inverse_ref, sum_ref, near_ref, wrap_ref, far_ref, mom_ref,
    fb_ref, mom_out_ref, right_ref,
    fb_buf, mom_buf, right_buf, fb_sem, mom_sem, right_sem,
):
    total = (sum_ref[...] + near_ref[...]) + (wrap_ref[...] + far_ref[...])
    pieces = []
    for start in range(0, COLS, LANES):
        piece = jnp.zeros((RANK, LANES), F32)
        for k in range(RANK):
            piece += inverse_ref[k * RANK : (k + 1) * RANK, :] * total[k : k + 1, start : start + LANES]
        pieces.append(piece)
    right = jnp.concatenate(pieces, axis=1)
    right_buf[...] = right
    copies = [pltpu.make_async_copy(right_buf, right_ref, right_sem.at[0])]
    copies[0].start()
    high, low = split(right, 2)
    pack = jnp.concatenate([high, low, high, low], axis=0)
    mine = own_half()
    for i, (start, count) in enumerate(WRITES):
        rows = pl.ds(start, count)
        merged_ref, half, low_row = (own_ref, mine, start) if start < HALF else (other_ref, 1 - mine, start - HALF)
        merged = merged_ref[pl.ds(low_row, count), :]
        approx = jnp.dot(basis_ref[rows, :], pack, preferred_element_type=F32)
        fb_buf[rows, :] = (merged.astype(F32) - approx).astype(BF16)
        target = fb_ref.at[0, pl.ds(pl.multiple_of(half * HALF + low_row, WRITES[0][1]), count), :]
        copies.append(pltpu.make_async_copy(fb_buf.at[rows, :], target, fb_sem.at[i]))
        copies[-1].start()
        if i == 0:
            count = mom_ref.shape[0]
            replica, per_half = lax.axis_index("replica"), HALF // count
            start = jnp.where(replica // per_half == mine, 0, HALF) + lax.rem(replica, per_half) * count
            mom_rows = pl.ds(pl.multiple_of(start, count), count)
            approx = jnp.dot(basis_ref[mom_rows, :], pack, preferred_element_type=F32)
            mom_buf[...] = (0.9 * mom_ref[...].astype(F32) + approx).astype(BF16)
            copies.append(pltpu.make_async_copy(mom_buf, mom_out_ref, mom_sem.at[0]))
            copies[-1].start()
    for copy in copies:
        copy.wait()


def finish(merged_own, merged_other, basis, inverse, parts, momentum):
    mom_rows = momentum.shape[0]
    return pl.pallas_call(
        final_kernel,
        in_specs=[whole()] * 9,
        out_specs=in_hbm(3),
        out_shape=[
            jax.ShapeDtypeStruct((1, ROWS, COLS), BF16),
            jax.ShapeDtypeStruct((mom_rows, COLS), BF16),
            jax.ShapeDtypeStruct((RANK, COLS), F32),
        ],
        scratch_shapes=[
            pltpu.VMEM((ROWS, COLS), BF16),
            pltpu.VMEM((mom_rows, COLS), BF16),
            pltpu.VMEM((RANK, COLS), F32),
            pltpu.SemaphoreType.DMA((len(WRITES),)),
            pltpu.SemaphoreType.DMA((1,)),
            pltpu.SemaphoreType.DMA((1,)),
        ],
        compiler_params=pltpu.CompilerParams(vmem_limit_bytes=20 * MIB),
        cost_estimate=pl.CostEstimate(flops=2 * ROWS * COLS * 32, bytes_accessed=4 * ROWS * COLS, transcendentals=0),
        name="finish",
    )(merged_own, merged_other, basis, inverse, *parts, momentum)


CORE, LOW = 16, {"y": 32, "z": 4, "x": 1}


def swap(x, masks):
    pairs = [(i, i ^ masks[i.bit_count() % 2]) for i in range(128)]
    return lax.ppermute(x, ("replica", "tensor"), pairs)


def ring_sum(x, axes):
    near = swap(x, [LOW[a] | CORE for a in axes])
    wrap = swap(x, [3 * LOW[a] for a in axes])
    return x + near + wrap + swap(x, [2 * LOW[a] | CORE for a in axes])


def sibling(x):
    return swap(x, [CORE] * 2)


def shards(gradient, feedback, momentum, right_init):
    gradient = pltpu.with_memory_space_constraint(gradient, pltpu.HBM)
    feedback = pltpu.with_memory_space_constraint(feedback, pltpu.HBM)
    right_t = pltpu.with_memory_space_constraint(right_init.T, pltpu.HBM)
    momentum = pltpu.with_memory_space_constraint(momentum, pltpu.VMEM)
    merged_other, send, *loaded = merge_other(gradient, feedback, right_t)
    received = sibling(send)
    merged_own, keep = merge_own(*loaded)
    own = keep + received
    for axes in ("yx", "xz", "zy"):
        own = ring_sum(own, axes)
    other = sibling(own)
    term = right_term(merged_other, other, right_term(merged_own, own))
    inverse, basis = make_basis(lax.axis_size("replica"), own, other)
    term = term + sibling(term)
    parts = [term, *(swap(term, [steps * LOW["y"] | CORE] * 2) for steps in (1, 3, 2))]
    feedback_out, momentum_out, right_t = finish(merged_own, merged_other, basis, inverse, parts, momentum)
    return feedback_out, momentum_out, right_t.T


def solution(mesh):
    placed = (
        P("replica", None, "tensor"),
        P("replica", None, "tensor"),
        P("replica", "tensor"),
        P("tensor", None),
    )
    return jax.shard_map(
        shards,
        mesh=mesh,
        in_specs=placed,
        out_specs=(P("replica", None, "tensor"), P("replica", "tensor"), P("tensor", None)),
        check_vma=False,
    )
```

```python
import jax
import jax.numpy as jnp
from jax import lax
from jax.experimental import pallas as pl
from jax.experimental.pallas import tpu as pltpu
from jax.sharding import PartitionSpec as P

F32, BF16 = jnp.float32, jnp.bfloat16
ROWS, COLS, RANK = 6144, 384, 8
HALF = ROWS // 2
CHUNKS = 3
CHUNK = HALF // CHUNKS
WRITES = [(start, HALF // 4) for start in range(0, ROWS, HALF // 4)]
LANES = 128
MIB = 1 << 20


def own_half():
    replica, tensor = lax.axis_index("replica"), lax.axis_index("tensor")
    bits = replica + replica // 2 + replica // 4 + tensor + tensor // 2 + tensor // 4 + tensor // 8
    return lax.rem(bits, 2)


def split(x, count):
    terms = []
    for _ in range(count):
        terms.append(x.astype(BF16))
        x = x - terms[-1].astype(F32)
    return terms


def merge_chunk(g_ref, f_ref, right, merged_ref, term_ref, i):
    here = pl.ds(i * CHUNK, CHUNK)
    merged = (g_ref[here, :].astype(F32) + f_ref[here, :].astype(F32)).astype(BF16)
    merged_ref[here, :] = merged
    term_ref[:, here] = lax.dot_general(right, merged, (((1,), (1,)), ((), ())), preferred_element_type=F32)


def load_pair(g_ref, f_ref, half, start, count, g_to, f_to, g_sem, f_sem):
    here, rows = pl.ds(start, count), pl.ds(pl.multiple_of(half * HALF + start, CHUNK), count)
    pair = (
        pltpu.make_async_copy(g_ref.at[0, rows, :], g_to.at[here, :], g_sem),
        pltpu.make_async_copy(f_ref.at[0, rows, :], f_to.at[here, :], f_sem),
    )
    for copy in pair:
        copy.start()
    return pair


def load_kernel(g_ref, f_ref, q_ref, merged_ref, term_ref, g_own, f_own, q_own, g_buf, f_buf, g_sem, f_sem, q_sem):
    mine = own_half()
    q_copy = pltpu.make_async_copy(q_ref, q_own, q_sem.at[0])
    q_copy.start()
    copies = [
        load_pair(g_ref, f_ref, 1 - mine, i * CHUNK, CHUNK, g_buf, f_buf, g_sem.at[i], f_sem.at[i]) for i in range(CHUNKS)
    ]
    copies.append(load_pair(g_ref, f_ref, mine, 0, HALF, g_own, f_own, g_sem.at[CHUNKS], f_sem.at[CHUNKS]))
    q_copy.wait()
    right = q_own[...].astype(BF16)
    for i, pair in enumerate(copies):
        for copy in pair:
            copy.wait()
        if i < CHUNKS:
            merge_chunk(g_buf, f_buf, right, merged_ref, term_ref, i)


def merge_kernel(g_ref, f_ref, q_ref, merged_ref, term_ref):
    right = q_ref[...].astype(BF16)
    for i in range(CHUNKS):
        merge_chunk(g_ref, f_ref, right, merged_ref, term_ref, i)


def whole():
    return pl.BlockSpec(memory_space=pltpu.VMEM)


def in_hbm(count):
    return [pl.BlockSpec(memory_space=pltpu.HBM)] * count


def merge_other(gradient, feedback, right_t):
    half_rows = pltpu.VMEM((HALF, COLS), BF16)
    return pl.pallas_call(
        load_kernel,
        in_specs=in_hbm(3),
        out_specs=[whole()] * 5,
        out_shape=[
            half_rows,
            pltpu.VMEM((RANK, HALF), F32),
            half_rows,
            half_rows,
            pltpu.VMEM((RANK, COLS), F32),
        ],
        scratch_shapes=[
            half_rows,
            half_rows,
            pltpu.SemaphoreType.DMA((CHUNKS + 1,)),
            pltpu.SemaphoreType.DMA((CHUNKS + 1,)),
            pltpu.SemaphoreType.DMA((1,)),
        ],
        compiler_params=pltpu.CompilerParams(vmem_limit_bytes=16 * MIB),
        cost_estimate=pl.CostEstimate(flops=HALF * COLS * RANK * 2, bytes_accessed=8 * HALF * COLS, transcendentals=0),
        name="merge_other",
    )(gradient, feedback, right_t)


def merge_own(gradient, feedback, right_t):
    return pl.pallas_call(
        merge_kernel,
        in_specs=[whole()] * 3,
        out_specs=[whole(), whole()],
        out_shape=[pltpu.VMEM((HALF, COLS), BF16), pltpu.VMEM((RANK, HALF), F32)],
        compiler_params=pltpu.CompilerParams(vmem_limit_bytes=16 * MIB),
        cost_estimate=pl.CostEstimate(flops=HALF * COLS * RANK * 2, bytes_accessed=4 * HALF * COLS, transcendentals=0),
        name="merge_own",
    )(gradient, feedback, right_t)


def right_kernel(merged_ref, left_ref, *refs):
    terms = jnp.concatenate(split(left_ref[...], 3), axis=0)
    total = jnp.dot(terms, merged_ref[...], preferred_element_type=F32)
    total = total[2 * RANK :] + total[RANK : 2 * RANK] + total[:RANK]
    for ref in refs[:-1]:
        total += ref[...]
    refs[-1][...] = total


def right_term(merged, left, *before):
    return pl.pallas_call(
        right_kernel,
        in_specs=[whole()] * (2 + len(before)),
        out_specs=whole(),
        out_shape=pltpu.VMEM((RANK, COLS), F32),
        compiler_params=pltpu.CompilerParams(vmem_limit_bytes=16 * MIB),
        cost_estimate=pl.CostEstimate(flops=4 * HALF * COLS * RANK, bytes_accessed=2 * HALF * COLS, transcendentals=0),
        name="right_other" if before else "right_own",
    )(merged, left, *before)


def basis_kernel(replicas, own_ref, other_ref, inverse_ref, basis_ref):
    own, other = own_ref[...], other_ref[...]
    gram = jnp.zeros((RANK, RANK), F32)
    for part in (own, other):
        gram += lax.dot_general(
            part, part, (((1,), (1,)), ((), ())), precision=lax.Precision.HIGHEST, preferred_element_type=F32
        )
    row = lax.broadcasted_iota(jnp.int32, (RANK, RANK), 0)
    column = lax.broadcasted_iota(jnp.int32, (RANK, RANK), 1)
    eye = jnp.where(row == column, 1.0, 0.0)
    inverse = eye
    for k in range(RANK):
        factor = jnp.where(row[:, :1] > k, gram[:, k : k + 1] / gram[k : k + 1, k : k + 1], 0.0)
        inverse -= factor * inverse[k : k + 1, :]
        gram -= factor * gram[k : k + 1, :]
    pivots = jnp.sum(gram * eye, axis=1, keepdims=True)
    inverse = inverse / jnp.sqrt(pivots)
    for k in range(RANK):
        column = inverse[:, k : k + 1] * (1.0 / replicas)
        inverse_ref[k * RANK : (k + 1) * RANK, :] = jnp.broadcast_to(column, (RANK, LANES))
    for part, start in ((own, 0), (other, HALF)):
        basis = jnp.zeros((RANK, HALF), F32)
        for k in range(RANK):
            basis += inverse[:, k : k + 1] * part[k : k + 1, :]
        high, low = split(basis, 2)
        packed = jnp.concatenate([high, high, low, low], axis=0)
        basis_ref[start : start + HALF, :] = packed.T


def make_basis(replicas, own, other):
    def body(*refs):
        basis_kernel(replicas, *refs)

    return pl.pallas_call(
        body,
        in_specs=[whole(), whole()],
        out_specs=[whole(), whole()],
        out_shape=[pltpu.VMEM((RANK * RANK, LANES), F32), pltpu.VMEM((ROWS, 4 * RANK), BF16)],
        compiler_params=pltpu.CompilerParams(vmem_limit_bytes=16 * MIB),
        cost_estimate=pl.CostEstimate(flops=4 * ROWS * RANK * RANK, bytes_accessed=4 * MIB, transcendentals=0),
        name="basis",
    )(own, other)


def final_kernel(
    own_ref, other_ref, basis_ref, inverse_ref, sum_ref, near_ref, wrap_ref, far_ref, mom_ref,
    fb_ref, mom_out_ref, right_ref,
    fb_buf, mom_buf, right_buf, fb_sem, mom_sem, right_sem,
):
    total = (sum_ref[...] + near_ref[...]) + (wrap_ref[...] + far_ref[...])
    pieces = []
    for start in range(0, COLS, LANES):
        piece = jnp.zeros((RANK, LANES), F32)
        for k in range(RANK):
            piece += inverse_ref[k * RANK : (k + 1) * RANK, :] * total[k : k + 1, start : start + LANES]
        pieces.append(piece)
    right = jnp.concatenate(pieces, axis=1)
    right_buf[...] = right
    copies = [pltpu.make_async_copy(right_buf, right_ref, right_sem.at[0])]
    copies[0].start()
    high, low = split(right, 2)
    pack = jnp.concatenate([high, low, high, low], axis=0)
    mine = own_half()
    for i, (start, count) in enumerate(WRITES):
        rows = pl.ds(start, count)
        merged_ref, half, low_row = (own_ref, mine, start) if start < HALF else (other_ref, 1 - mine, start - HALF)
        merged = merged_ref[pl.ds(low_row, count), :]
        approx = jnp.dot(basis_ref[rows, :], pack, preferred_element_type=F32)
        fb_buf[rows, :] = (merged.astype(F32) - approx).astype(BF16)
        target = fb_ref.at[0, pl.ds(pl.multiple_of(half * HALF + low_row, WRITES[0][1]), count), :]
        copies.append(pltpu.make_async_copy(fb_buf.at[rows, :], target, fb_sem.at[i]))
        copies[-1].start()
        if i == 0:
            count = mom_ref.shape[0]
            replica, per_half = lax.axis_index("replica"), HALF // count
            start = jnp.where(replica // per_half == mine, 0, HALF) + lax.rem(replica, per_half) * count
            mom_rows = pl.ds(pl.multiple_of(start, count), count)
            approx = jnp.dot(basis_ref[mom_rows, :], pack, preferred_element_type=F32)
            mom_buf[...] = (0.9 * mom_ref[...].astype(F32) + approx).astype(BF16)
            copies.append(pltpu.make_async_copy(mom_buf, mom_out_ref, mom_sem.at[0]))
            copies[-1].start()
    for copy in copies:
        copy.wait()


def finish(merged_own, merged_other, basis, inverse, parts, momentum):
    mom_rows = momentum.shape[0]
    return pl.pallas_call(
        final_kernel,
        in_specs=[whole()] * 9,
        out_specs=in_hbm(3),
        out_shape=[
            jax.ShapeDtypeStruct((1, ROWS, COLS), BF16),
            jax.ShapeDtypeStruct((mom_rows, COLS), BF16),
            jax.ShapeDtypeStruct((RANK, COLS), F32),
        ],
        scratch_shapes=[
            pltpu.VMEM((ROWS, COLS), BF16),
            pltpu.VMEM((mom_rows, COLS), BF16),
            pltpu.VMEM((RANK, COLS), F32),
            pltpu.SemaphoreType.DMA((len(WRITES),)),
            pltpu.SemaphoreType.DMA((1,)),
            pltpu.SemaphoreType.DMA((1,)),
        ],
        compiler_params=pltpu.CompilerParams(vmem_limit_bytes=20 * MIB),
        cost_estimate=pl.CostEstimate(flops=2 * ROWS * COLS * 32, bytes_accessed=4 * ROWS * COLS, transcendentals=0),
        name="finish",
    )(merged_own, merged_other, basis, inverse, *parts, momentum)


CORE, LOW = 16, {"y": 32, "z": 4, "x": 1}


def swap(x, masks):
    pairs = [(i, i ^ masks[i.bit_count() % 2]) for i in range(128)]
    return lax.ppermute(x, ("replica", "tensor"), pairs)


def ring_sum(x, axes):
    near = swap(x, [LOW[a] | CORE for a in axes])
    wrap = swap(x, [3 * LOW[a] for a in axes])
    return x + near + wrap + swap(x, [2 * LOW[a] | CORE for a in axes])


def sibling(x):
    return swap(x, [CORE] * 2)


def shards(gradient, feedback, momentum, right_init):
    gradient = pltpu.with_memory_space_constraint(gradient, pltpu.HBM)
    feedback = pltpu.with_memory_space_constraint(feedback, pltpu.HBM)
    right_t = pltpu.with_memory_space_constraint(right_init.T, pltpu.HBM)
    momentum = pltpu.with_memory_space_constraint(momentum, pltpu.VMEM)
    merged_other, send, *loaded = merge_other(gradient, feedback, right_t)
    received = sibling(send)
    merged_own, keep = merge_own(*loaded)
    own = keep + received
    for axes in ("yx", "xz", "zy"):
        own = ring_sum(own, axes)
    other = sibling(own)
    term = right_term(merged_other, other, right_term(merged_own, own))
    inverse, basis = make_basis(lax.axis_size("replica"), own, other)
    term = term + sibling(term)
    parts = [term, *(swap(term, [steps * LOW["y"] | CORE] * 2) for steps in (1, 3, 2))]
    feedback_out, momentum_out, right_t = finish(merged_own, merged_other, basis, inverse, parts, momentum)
    return feedback_out, momentum_out, right_t.T


def solution(mesh):
    placed = (
        P("replica", None, "tensor"),
        P("replica", None, "tensor"),
        P("replica", "tensor"),
        P("tensor", None),
    )
    return jax.shard_map(
        shards,
        mesh=mesh,
        in_specs=placed,
        out_specs=(P("replica", None, "tensor"), P("replica", "tensor"), P("tensor", None)),
        check_vma=False,
    )
```

```python
import jax
import jax.numpy as jnp
from jax import lax
from jax.experimental import pallas as pl
from jax.experimental.pallas import tpu as pltpu
from jax.sharding import PartitionSpec as P

F32, BF16 = jnp.float32, jnp.bfloat16
ROWS, COLS, RANK = 6144, 384, 8
HALF = ROWS // 2
CHUNKS = 3
CHUNK = HALF // CHUNKS
WRITES = [(start, HALF // 4) for start in range(0, ROWS, HALF // 4)]
LANES = 128
MIB = 1 << 20


def own_half():
    replica, tensor = lax.axis_index("replica"), lax.axis_index("tensor")
    bits = replica + replica // 2 + replica // 4 + tensor + tensor // 2 + tensor // 4 + tensor // 8
    return lax.rem(bits, 2)


def split(x, count):
    terms = []
    for _ in range(count):
        terms.append(x.astype(BF16))
        x = x - terms[-1].astype(F32)
    return terms


def rows_of(half, chunk):
    return pl.ds(pl.multiple_of(half * HALF + chunk * CHUNK, CHUNK), CHUNK)


def merge_chunk(g_ref, f_ref, right, merged_ref, term_ref, i):
    here = pl.ds(i * CHUNK, CHUNK)
    merged = (g_ref[here, :].astype(F32) + f_ref[here, :].astype(F32)).astype(BF16)
    merged_ref[here, :] = merged
    term_ref[:, here] = lax.dot_general(right, merged, (((1,), (1,)), ((), ())), preferred_element_type=F32)


def load_pair(g_ref, f_ref, half, i, g_to, f_to, g_sem, f_sem):
    here = pl.ds(i * CHUNK, CHUNK)
    pair = (
        pltpu.make_async_copy(g_ref.at[0, rows_of(half, i), :], g_to.at[here, :], g_sem),
        pltpu.make_async_copy(f_ref.at[0, rows_of(half, i), :], f_to.at[here, :], f_sem),
    )
    for copy in pair:
        copy.start()
    return pair


def load_kernel(g_ref, f_ref, q_ref, merged_ref, term_ref, g_own, f_own, q_own, g_buf, f_buf, g_sem, f_sem, q_sem):
    mine = own_half()
    q_copy = pltpu.make_async_copy(q_ref, q_own, q_sem.at[0])
    q_copy.start()
    copies = []
    for half, g_to, f_to in ((1 - mine, g_buf, f_buf), (mine, g_own, f_own)):
        for i in range(CHUNKS):
            n = len(copies)
            copies.append(load_pair(g_ref, f_ref, half, i, g_to, f_to, g_sem.at[n], f_sem.at[n]))
    q_copy.wait()
    right = q_own[...].astype(BF16)
    for i, pair in enumerate(copies):
        for copy in pair:
            copy.wait()
        if i < CHUNKS:
            merge_chunk(g_buf, f_buf, right, merged_ref, term_ref, i)


def merge_kernel(g_ref, f_ref, q_ref, merged_ref, term_ref):
    right = q_ref[...].astype(BF16)
    for i in range(CHUNKS):
        merge_chunk(g_ref, f_ref, right, merged_ref, term_ref, i)


def whole():
    return pl.BlockSpec(memory_space=pltpu.VMEM)


def in_hbm(count):
    return [pl.BlockSpec(memory_space=pltpu.HBM)] * count


def merge_other(gradient, feedback, right_t):
    half_rows = pltpu.VMEM((HALF, COLS), BF16)
    return pl.pallas_call(
        load_kernel,
        in_specs=in_hbm(3),
        out_specs=[whole()] * 5,
        out_shape=[
            half_rows,
            pltpu.VMEM((RANK, HALF), F32),
            half_rows,
            half_rows,
            pltpu.VMEM((RANK, COLS), F32),
        ],
        scratch_shapes=[
            half_rows,
            half_rows,
            pltpu.SemaphoreType.DMA((2 * CHUNKS,)),
            pltpu.SemaphoreType.DMA((2 * CHUNKS,)),
            pltpu.SemaphoreType.DMA((1,)),
        ],
        compiler_params=pltpu.CompilerParams(vmem_limit_bytes=16 * MIB),
        cost_estimate=pl.CostEstimate(flops=HALF * COLS * RANK * 2, bytes_accessed=8 * HALF * COLS, transcendentals=0),
        name="merge_other",
    )(gradient, feedback, right_t)


def merge_own(gradient, feedback, right_t):
    return pl.pallas_call(
        merge_kernel,
        in_specs=[whole()] * 3,
        out_specs=[whole(), whole()],
        out_shape=[pltpu.VMEM((HALF, COLS), BF16), pltpu.VMEM((RANK, HALF), F32)],
        compiler_params=pltpu.CompilerParams(vmem_limit_bytes=16 * MIB),
        cost_estimate=pl.CostEstimate(flops=HALF * COLS * RANK * 2, bytes_accessed=4 * HALF * COLS, transcendentals=0),
        name="merge_own",
    )(gradient, feedback, right_t)


def right_kernel(merged_ref, left_ref, *refs):
    terms = jnp.concatenate(split(left_ref[...], 3), axis=0)
    total = jnp.dot(terms, merged_ref[...], preferred_element_type=F32)
    total = total[2 * RANK :] + total[RANK : 2 * RANK] + total[:RANK]
    for ref in refs[:-1]:
        total += ref[...]
    refs[-1][...] = total


def right_term(merged, left, *before):
    return pl.pallas_call(
        right_kernel,
        in_specs=[whole()] * (2 + len(before)),
        out_specs=whole(),
        out_shape=pltpu.VMEM((RANK, COLS), F32),
        compiler_params=pltpu.CompilerParams(vmem_limit_bytes=16 * MIB),
        cost_estimate=pl.CostEstimate(flops=4 * HALF * COLS * RANK, bytes_accessed=2 * HALF * COLS, transcendentals=0),
        name="right_other" if before else "right_own",
    )(merged, left, *before)


def basis_kernel(replicas, own_ref, other_ref, inverse_ref, basis_ref):
    own, other = own_ref[...], other_ref[...]
    gram = jnp.zeros((RANK, RANK), F32)
    for part in (own, other):
        gram += lax.dot_general(
            part, part, (((1,), (1,)), ((), ())), precision=lax.Precision.HIGHEST, preferred_element_type=F32
        )
    row = lax.broadcasted_iota(jnp.int32, (RANK, RANK), 0)
    column = lax.broadcasted_iota(jnp.int32, (RANK, RANK), 1)
    eye = jnp.where(row == column, 1.0, 0.0)
    inverse = eye
    for k in range(RANK):
        factor = jnp.where(row[:, :1] > k, gram[:, k : k + 1] / gram[k : k + 1, k : k + 1], 0.0)
        inverse -= factor * inverse[k : k + 1, :]
        gram -= factor * gram[k : k + 1, :]
    pivots = jnp.sum(gram * eye, axis=1, keepdims=True)
    inverse = inverse / jnp.sqrt(pivots)
    for k in range(RANK):
        column = inverse[:, k : k + 1] * (1.0 / replicas)
        inverse_ref[k * RANK : (k + 1) * RANK, :] = jnp.broadcast_to(column, (RANK, LANES))
    for part, start in ((own, 0), (other, HALF)):
        basis = jnp.zeros((RANK, HALF), F32)
        for k in range(RANK):
            basis += inverse[:, k : k + 1] * part[k : k + 1, :]
        high, low = split(basis, 2)
        packed = jnp.concatenate([high, high, low, low], axis=0)
        basis_ref[start : start + HALF, :] = packed.T


def make_basis(replicas, own, other):
    def body(*refs):
        basis_kernel(replicas, *refs)

    return pl.pallas_call(
        body,
        in_specs=[whole(), whole()],
        out_specs=[whole(), whole()],
        out_shape=[pltpu.VMEM((RANK * RANK, LANES), F32), pltpu.VMEM((ROWS, 4 * RANK), BF16)],
        compiler_params=pltpu.CompilerParams(vmem_limit_bytes=16 * MIB),
        cost_estimate=pl.CostEstimate(flops=4 * ROWS * RANK * RANK, bytes_accessed=4 * MIB, transcendentals=0),
        name="basis",
    )(own, other)


def final_kernel(
    own_ref, other_ref, basis_ref, inverse_ref, sum_ref, sibling_ref, mom_ref,
    fb_ref, mom_out_ref, right_ref,
    fb_buf, mom_buf, right_buf, fb_sem, mom_sem, right_sem,
):
    total = sum_ref[...] + sibling_ref[...]
    pieces = []
    for start in range(0, COLS, LANES):
        piece = jnp.zeros((RANK, LANES), F32)
        for k in range(RANK):
            piece += inverse_ref[k * RANK : (k + 1) * RANK, :] * total[k : k + 1, start : start + LANES]
        pieces.append(piece)
    right = jnp.concatenate(pieces, axis=1)
    right_buf[...] = right
    copies = [pltpu.make_async_copy(right_buf, right_ref, right_sem.at[0])]
    copies[0].start()
    high, low = split(right, 2)
    pack = jnp.concatenate([high, low, high, low], axis=0)
    mine = own_half()
    for i, (start, count) in enumerate(WRITES):
        rows = pl.ds(start, count)
        merged_ref, half, low_row = (own_ref, mine, start) if start < HALF else (other_ref, 1 - mine, start - HALF)
        merged = merged_ref[pl.ds(low_row, count), :]
        approx = jnp.dot(basis_ref[rows, :], pack, preferred_element_type=F32)
        fb_buf[rows, :] = (merged.astype(F32) - approx).astype(BF16)
        target = fb_ref.at[0, pl.ds(pl.multiple_of(half * HALF + low_row, WRITES[0][1]), count), :]
        copies.append(pltpu.make_async_copy(fb_buf.at[rows, :], target, fb_sem.at[i]))
        copies[-1].start()
        if i == 0:
            count = mom_ref.shape[0]
            replica, per_half = lax.axis_index("replica"), HALF // count
            start = jnp.where(replica // per_half == mine, 0, HALF) + lax.rem(replica, per_half) * count
            mom_rows = pl.ds(pl.multiple_of(start, count), count)
            approx = jnp.dot(basis_ref[mom_rows, :], pack, preferred_element_type=F32)
            mom_buf[...] = (0.9 * mom_ref[...].astype(F32) + approx).astype(BF16)
            copies.append(pltpu.make_async_copy(mom_buf, mom_out_ref, mom_sem.at[0]))
            copies[-1].start()
    for copy in copies:
        copy.wait()


def finish(merged_own, merged_other, basis, inverse, parts, momentum):
    mom_rows = momentum.shape[0]
    return pl.pallas_call(
        final_kernel,
        in_specs=[whole()] * 7,
        out_specs=in_hbm(3),
        out_shape=[
            jax.ShapeDtypeStruct((1, ROWS, COLS), BF16),
            jax.ShapeDtypeStruct((mom_rows, COLS), BF16),
            jax.ShapeDtypeStruct((RANK, COLS), F32),
        ],
        scratch_shapes=[
            pltpu.VMEM((ROWS, COLS), BF16),
            pltpu.VMEM((mom_rows, COLS), BF16),
            pltpu.VMEM((RANK, COLS), F32),
            pltpu.SemaphoreType.DMA((len(WRITES),)),
            pltpu.SemaphoreType.DMA((1,)),
            pltpu.SemaphoreType.DMA((1,)),
        ],
        compiler_params=pltpu.CompilerParams(vmem_limit_bytes=20 * MIB),
        cost_estimate=pl.CostEstimate(flops=2 * ROWS * COLS * 32, bytes_accessed=4 * ROWS * COLS, transcendentals=0),
        name="finish",
    )(merged_own, merged_other, basis, inverse, *parts, momentum)


CORE, LOW = 16, {"y": 32, "z": 4, "x": 1}


def swap(x, masks):
    pairs = [(i, i ^ masks[i.bit_count() % 2]) for i in range(128)]
    return lax.ppermute(x, ("replica", "tensor"), pairs)


def ring_sum(x, axes):
    near = swap(x, [LOW[a] | CORE for a in axes])
    wrap = swap(x, [3 * LOW[a] for a in axes])
    return x + near + wrap + swap(x, [2 * LOW[a] | CORE for a in axes])


def sibling(x):
    return swap(x, [CORE] * 2)


def shards(gradient, feedback, momentum, right_init):
    gradient = pltpu.with_memory_space_constraint(gradient, pltpu.HBM)
    feedback = pltpu.with_memory_space_constraint(feedback, pltpu.HBM)
    right_t = pltpu.with_memory_space_constraint(right_init.T, pltpu.HBM)
    momentum = pltpu.with_memory_space_constraint(momentum, pltpu.VMEM)
    merged_other, send, *loaded = merge_other(gradient, feedback, right_t)
    received = sibling(send)
    merged_own, keep = merge_own(*loaded)
    own = keep + received
    for axes in ("yx", "xz", "zy"):
        own = ring_sum(own, axes)
    other = sibling(own)
    term = right_term(merged_other, other, right_term(merged_own, own))
    inverse, basis = make_basis(lax.axis_size("replica"), own, other)
    near, wrap, far = (swap(term, [steps * LOW["y"] | CORE] * 2) for steps in (1, 3, 2))
    term = term + near + wrap + far
    parts = [term, sibling(term)]
    feedback_out, momentum_out, right_t = finish(merged_own, merged_other, basis, inverse, parts, momentum)
    return feedback_out, momentum_out, right_t.T


def solution(mesh):
    placed = (
        P("replica", None, "tensor"),
        P("replica", None, "tensor"),
        P("replica", "tensor"),
        P("tensor", None),
    )
    return jax.shard_map(
        shards,
        mesh=mesh,
        in_specs=placed,
        out_specs=(P("replica", None, "tensor"), P("replica", "tensor"), P("tensor", None)),
        check_vma=False,
    )
```

```python
import jax
import jax.numpy as jnp
from jax import lax
from jax.experimental import pallas as pl
from jax.experimental.pallas import tpu as pltpu
from jax.sharding import PartitionSpec as P

F32, BF16 = jnp.float32, jnp.bfloat16
ROWS, COLS, RANK = 6144, 384, 8
HALF = ROWS // 2
CHUNKS = 4
CHUNK = HALF // CHUNKS
WRITES = [(start, HALF // 4) for start in range(0, ROWS, HALF // 4)]
LANES = 128
MIB = 1 << 20


def own_half():
    replica, tensor = lax.axis_index("replica"), lax.axis_index("tensor")
    bits = replica + replica // 2 + replica // 4 + tensor + tensor // 2 + tensor // 4 + tensor // 8
    return lax.rem(bits, 2)


def split(x, count):
    terms = []
    for _ in range(count):
        terms.append(x.astype(BF16))
        x = x - terms[-1].astype(F32)
    return terms


def rows_of(half, chunk):
    return pl.ds(pl.multiple_of(half * HALF + chunk * CHUNK, CHUNK), CHUNK)


def merge_chunk(g_ref, f_ref, right, merged_ref, term_ref, i):
    here = pl.ds(i * CHUNK, CHUNK)
    merged = (g_ref[here, :].astype(F32) + f_ref[here, :].astype(F32)).astype(BF16)
    merged_ref[here, :] = merged
    term_ref[:, here] = lax.dot_general(right, merged, (((1,), (1,)), ((), ())), preferred_element_type=F32)


def load_pair(g_ref, f_ref, half, i, g_to, f_to, g_sem, f_sem):
    here = pl.ds(i * CHUNK, CHUNK)
    pair = (
        pltpu.make_async_copy(g_ref.at[0, rows_of(half, i), :], g_to.at[here, :], g_sem),
        pltpu.make_async_copy(f_ref.at[0, rows_of(half, i), :], f_to.at[here, :], f_sem),
    )
    for copy in pair:
        copy.start()
    return pair


def load_kernel(g_ref, f_ref, q_ref, merged_ref, term_ref, g_own, f_own, q_own, g_buf, f_buf, g_sem, f_sem, q_sem):
    mine = own_half()
    q_copy = pltpu.make_async_copy(q_ref, q_own, q_sem.at[0])
    q_copy.start()
    copies = []
    for half, g_to, f_to in ((1 - mine, g_buf, f_buf), (mine, g_own, f_own)):
        for i in range(CHUNKS):
            n = len(copies)
            copies.append(load_pair(g_ref, f_ref, half, i, g_to, f_to, g_sem.at[n], f_sem.at[n]))
    q_copy.wait()
    right = q_own[...].astype(BF16)
    for i, pair in enumerate(copies):
        for copy in pair:
            copy.wait()
        if i < CHUNKS:
            merge_chunk(g_buf, f_buf, right, merged_ref, term_ref, i)


def merge_kernel(g_ref, f_ref, q_ref, merged_ref, term_ref):
    right = q_ref[...].astype(BF16)
    for i in range(CHUNKS):
        merge_chunk(g_ref, f_ref, right, merged_ref, term_ref, i)


def whole():
    return pl.BlockSpec(memory_space=pltpu.VMEM)


def in_hbm(count):
    return [pl.BlockSpec(memory_space=pltpu.HBM)] * count


def merge_other(gradient, feedback, right_t):
    half_rows = pltpu.VMEM((HALF, COLS), BF16)
    return pl.pallas_call(
        load_kernel,
        in_specs=in_hbm(3),
        out_specs=[whole()] * 5,
        out_shape=[
            half_rows,
            pltpu.VMEM((RANK, HALF), F32),
            half_rows,
            half_rows,
            pltpu.VMEM((RANK, COLS), F32),
        ],
        scratch_shapes=[
            half_rows,
            half_rows,
            pltpu.SemaphoreType.DMA((2 * CHUNKS,)),
            pltpu.SemaphoreType.DMA((2 * CHUNKS,)),
            pltpu.SemaphoreType.DMA((1,)),
        ],
        compiler_params=pltpu.CompilerParams(vmem_limit_bytes=16 * MIB),
        cost_estimate=pl.CostEstimate(flops=HALF * COLS * RANK * 2, bytes_accessed=8 * HALF * COLS, transcendentals=0),
        name="merge_other",
    )(gradient, feedback, right_t)


def merge_own(gradient, feedback, right_t):
    return pl.pallas_call(
        merge_kernel,
        in_specs=[whole()] * 3,
        out_specs=[whole(), whole()],
        out_shape=[pltpu.VMEM((HALF, COLS), BF16), pltpu.VMEM((RANK, HALF), F32)],
        compiler_params=pltpu.CompilerParams(vmem_limit_bytes=16 * MIB),
        cost_estimate=pl.CostEstimate(flops=HALF * COLS * RANK * 2, bytes_accessed=4 * HALF * COLS, transcendentals=0),
        name="merge_own",
    )(gradient, feedback, right_t)


def right_kernel(merged_ref, left_ref, *refs):
    terms = jnp.concatenate(split(left_ref[...], 3), axis=0)
    total = jnp.dot(terms, merged_ref[...], preferred_element_type=F32)
    total = total[2 * RANK :] + total[RANK : 2 * RANK] + total[:RANK]
    for ref in refs[:-1]:
        total += ref[...]
    refs[-1][...] = total


def right_term(merged, left, *before):
    return pl.pallas_call(
        right_kernel,
        in_specs=[whole()] * (2 + len(before)),
        out_specs=whole(),
        out_shape=pltpu.VMEM((RANK, COLS), F32),
        compiler_params=pltpu.CompilerParams(vmem_limit_bytes=16 * MIB),
        cost_estimate=pl.CostEstimate(flops=4 * HALF * COLS * RANK, bytes_accessed=2 * HALF * COLS, transcendentals=0),
        name="right_other" if before else "right_own",
    )(merged, left, *before)


def basis_kernel(replicas, own_ref, other_ref, inverse_ref, basis_ref):
    own, other = own_ref[...], other_ref[...]
    gram = jnp.zeros((RANK, RANK), F32)
    for part in (own, other):
        gram += lax.dot_general(
            part, part, (((1,), (1,)), ((), ())), precision=lax.Precision.HIGHEST, preferred_element_type=F32
        )
    row = lax.broadcasted_iota(jnp.int32, (RANK, RANK), 0)
    column = lax.broadcasted_iota(jnp.int32, (RANK, RANK), 1)
    eye = jnp.where(row == column, 1.0, 0.0)
    inverse = eye
    for k in range(RANK):
        factor = jnp.where(row[:, :1] > k, gram[:, k : k + 1] / gram[k : k + 1, k : k + 1], 0.0)
        inverse -= factor * inverse[k : k + 1, :]
        gram -= factor * gram[k : k + 1, :]
    pivots = jnp.sum(gram * eye, axis=1, keepdims=True)
    inverse = inverse / jnp.sqrt(pivots)
    for k in range(RANK):
        column = inverse[:, k : k + 1] * (1.0 / replicas)
        inverse_ref[k * RANK : (k + 1) * RANK, :] = jnp.broadcast_to(column, (RANK, LANES))
    for part, start in ((own, 0), (other, HALF)):
        basis = jnp.zeros((RANK, HALF), F32)
        for k in range(RANK):
            basis += inverse[:, k : k + 1] * part[k : k + 1, :]
        high, low = split(basis, 2)
        packed = jnp.concatenate([high, high, low, low], axis=0)
        basis_ref[start : start + HALF, :] = packed.T


def make_basis(replicas, own, other):
    def body(*refs):
        basis_kernel(replicas, *refs)

    return pl.pallas_call(
        body,
        in_specs=[whole(), whole()],
        out_specs=[whole(), whole()],
        out_shape=[pltpu.VMEM((RANK * RANK, LANES), F32), pltpu.VMEM((ROWS, 4 * RANK), BF16)],
        compiler_params=pltpu.CompilerParams(vmem_limit_bytes=16 * MIB),
        cost_estimate=pl.CostEstimate(flops=4 * ROWS * RANK * RANK, bytes_accessed=4 * MIB, transcendentals=0),
        name="basis",
    )(own, other)


def final_kernel(
    own_ref, other_ref, basis_ref, inverse_ref, sum_ref, near_ref, wrap_ref, far_ref, mom_ref,
    fb_ref, mom_out_ref, right_ref,
    fb_buf, mom_buf, right_buf, fb_sem, mom_sem, right_sem,
):
    total = (sum_ref[...] + near_ref[...]) + (wrap_ref[...] + far_ref[...])
    pieces = []
    for start in range(0, COLS, LANES):
        piece = jnp.zeros((RANK, LANES), F32)
        for k in range(RANK):
            piece += inverse_ref[k * RANK : (k + 1) * RANK, :] * total[k : k + 1, start : start + LANES]
        pieces.append(piece)
    right = jnp.concatenate(pieces, axis=1)
    right_buf[...] = right
    copies = [pltpu.make_async_copy(right_buf, right_ref, right_sem.at[0])]
    copies[0].start()
    high, low = split(right, 2)
    pack = jnp.concatenate([high, low, high, low], axis=0)
    mine = own_half()
    for i, (start, count) in enumerate(WRITES):
        rows = pl.ds(start, count)
        merged_ref, half, low_row = (own_ref, mine, start) if start < HALF else (other_ref, 1 - mine, start - HALF)
        merged = merged_ref[pl.ds(low_row, count), :]
        approx = jnp.dot(basis_ref[rows, :], pack, preferred_element_type=F32)
        fb_buf[rows, :] = (merged.astype(F32) - approx).astype(BF16)
        target = fb_ref.at[0, pl.ds(pl.multiple_of(half * HALF + low_row, WRITES[0][1]), count), :]
        copies.append(pltpu.make_async_copy(fb_buf.at[rows, :], target, fb_sem.at[i]))
        copies[-1].start()
        if i == 0:
            count = mom_ref.shape[0]
            replica, per_half = lax.axis_index("replica"), HALF // count
            start = jnp.where(replica // per_half == mine, 0, HALF) + lax.rem(replica, per_half) * count
            mom_rows = pl.ds(pl.multiple_of(start, count), count)
            approx = jnp.dot(basis_ref[mom_rows, :], pack, preferred_element_type=F32)
            mom_buf[...] = (0.9 * mom_ref[...].astype(F32) + approx).astype(BF16)
            copies.append(pltpu.make_async_copy(mom_buf, mom_out_ref, mom_sem.at[0]))
            copies[-1].start()
    for copy in copies:
        copy.wait()


def finish(merged_own, merged_other, basis, inverse, parts, momentum):
    mom_rows = momentum.shape[0]
    return pl.pallas_call(
        final_kernel,
        in_specs=[whole()] * 9,
        out_specs=in_hbm(3),
        out_shape=[
            jax.ShapeDtypeStruct((1, ROWS, COLS), BF16),
            jax.ShapeDtypeStruct((mom_rows, COLS), BF16),
            jax.ShapeDtypeStruct((RANK, COLS), F32),
        ],
        scratch_shapes=[
            pltpu.VMEM((ROWS, COLS), BF16),
            pltpu.VMEM((mom_rows, COLS), BF16),
            pltpu.VMEM((RANK, COLS), F32),
            pltpu.SemaphoreType.DMA((len(WRITES),)),
            pltpu.SemaphoreType.DMA((1,)),
            pltpu.SemaphoreType.DMA((1,)),
        ],
        compiler_params=pltpu.CompilerParams(vmem_limit_bytes=20 * MIB),
        cost_estimate=pl.CostEstimate(flops=2 * ROWS * COLS * 32, bytes_accessed=4 * ROWS * COLS, transcendentals=0),
        name="finish",
    )(merged_own, merged_other, basis, inverse, *parts, momentum)


CORE, LOW = 16, {"y": 32, "z": 4, "x": 1}


def swap(x, masks):
    pairs = [(i, i ^ masks[i.bit_count() % 2]) for i in range(128)]
    return lax.ppermute(x, ("replica", "tensor"), pairs)


def ring_sum(x, axes):
    near = swap(x, [LOW[a] | CORE for a in axes])
    wrap = swap(x, [3 * LOW[a] for a in axes])
    return x + near + wrap + swap(x, [2 * LOW[a] | CORE for a in axes])


def sibling(x):
    return swap(x, [CORE] * 2)


def shards(gradient, feedback, momentum, right_init):
    gradient = pltpu.with_memory_space_constraint(gradient, pltpu.HBM)
    feedback = pltpu.with_memory_space_constraint(feedback, pltpu.HBM)
    right_t = pltpu.with_memory_space_constraint(right_init.T, pltpu.HBM)
    momentum = pltpu.with_memory_space_constraint(momentum, pltpu.VMEM)
    merged_other, send, *loaded = merge_other(gradient, feedback, right_t)
    received = sibling(send)
    merged_own, keep = merge_own(*loaded)
    own = keep + received
    for axes in ("yx", "xz", "zy"):
        own = ring_sum(own, axes)
    other = sibling(own)
    term = right_term(merged_other, other, right_term(merged_own, own))
    inverse, basis = make_basis(lax.axis_size("replica"), own, other)
    term = term + sibling(term)
    parts = [term, *(swap(term, [steps * LOW["y"] | CORE] * 2) for steps in (1, 3, 2))]
    feedback_out, momentum_out, right_t = finish(merged_own, merged_other, basis, inverse, parts, momentum)
    return feedback_out, momentum_out, right_t.T


def solution(mesh):
    placed = (
        P("replica", None, "tensor"),
        P("replica", None, "tensor"),
        P("replica", "tensor"),
        P("tensor", None),
    )
    return jax.shard_map(
        shards,
        mesh=mesh,
        in_specs=placed,
        out_specs=(P("replica", None, "tensor"), P("replica", "tensor"), P("tensor", None)),
        check_vma=False,
    )
```

```python
import jax
import jax.numpy as jnp
from jax import lax
from jax.experimental import pallas as pl
from jax.experimental.pallas import tpu as pltpu
from jax.sharding import PartitionSpec as P

F32, BF16 = jnp.float32, jnp.bfloat16
ROWS, COLS, RANK = 6144, 384, 8
HALF = ROWS // 2
CHUNKS = 2
CHUNK = HALF // CHUNKS
WRITES = [(start, HALF // 4) for start in range(0, ROWS, HALF // 4)]
LANES = 128
MIB = 1 << 20


def own_half():
    replica, tensor = lax.axis_index("replica"), lax.axis_index("tensor")
    bits = replica + replica // 2 + replica // 4 + tensor + tensor // 2 + tensor // 4 + tensor // 8
    return lax.rem(bits, 2)


def split(x, count):
    terms = []
    for _ in range(count):
        terms.append(x.astype(BF16))
        x = x - terms[-1].astype(F32)
    return terms


def rows_of(half, chunk):
    return pl.ds(pl.multiple_of(half * HALF + chunk * CHUNK, CHUNK), CHUNK)


def merge_chunk(g_ref, f_ref, right, merged_ref, term_ref, i):
    here = pl.ds(i * CHUNK, CHUNK)
    merged = (g_ref[here, :].astype(F32) + f_ref[here, :].astype(F32)).astype(BF16)
    merged_ref[here, :] = merged
    term_ref[:, here] = lax.dot_general(right, merged, (((1,), (1,)), ((), ())), preferred_element_type=F32)


def load_pair(g_ref, f_ref, half, i, g_to, f_to, g_sem, f_sem):
    here = pl.ds(i * CHUNK, CHUNK)
    pair = (
        pltpu.make_async_copy(g_ref.at[0, rows_of(half, i), :], g_to.at[here, :], g_sem),
        pltpu.make_async_copy(f_ref.at[0, rows_of(half, i), :], f_to.at[here, :], f_sem),
    )
    for copy in pair:
        copy.start()
    return pair


def load_kernel(g_ref, f_ref, q_ref, merged_ref, term_ref, g_own, f_own, q_own, g_buf, f_buf, g_sem, f_sem, q_sem):
    mine = own_half()
    q_copy = pltpu.make_async_copy(q_ref, q_own, q_sem.at[0])
    q_copy.start()
    copies = []
    for half, g_to, f_to in ((1 - mine, g_buf, f_buf), (mine, g_own, f_own)):
        for i in range(CHUNKS):
            n = len(copies)
            copies.append(load_pair(g_ref, f_ref, half, i, g_to, f_to, g_sem.at[n], f_sem.at[n]))
    q_copy.wait()
    right = q_own[...].astype(BF16)
    for i, pair in enumerate(copies):
        for copy in pair:
            copy.wait()
        if i < CHUNKS:
            merge_chunk(g_buf, f_buf, right, merged_ref, term_ref, i)


def merge_kernel(g_ref, f_ref, q_ref, merged_ref, term_ref):
    right = q_ref[...].astype(BF16)
    for i in range(CHUNKS):
        merge_chunk(g_ref, f_ref, right, merged_ref, term_ref, i)


def whole():
    return pl.BlockSpec(memory_space=pltpu.VMEM)


def in_hbm(count):
    return [pl.BlockSpec(memory_space=pltpu.HBM)] * count


def merge_other(gradient, feedback, right_t):
    half_rows = pltpu.VMEM((HALF, COLS), BF16)
    return pl.pallas_call(
        load_kernel,
        in_specs=in_hbm(3),
        out_specs=[whole()] * 5,
        out_shape=[
            half_rows,
            pltpu.VMEM((RANK, HALF), F32),
            half_rows,
            half_rows,
            pltpu.VMEM((RANK, COLS), F32),
        ],
        scratch_shapes=[
            half_rows,
            half_rows,
            pltpu.SemaphoreType.DMA((2 * CHUNKS,)),
            pltpu.SemaphoreType.DMA((2 * CHUNKS,)),
            pltpu.SemaphoreType.DMA((1,)),
        ],
        compiler_params=pltpu.CompilerParams(vmem_limit_bytes=16 * MIB),
        cost_estimate=pl.CostEstimate(flops=HALF * COLS * RANK * 2, bytes_accessed=8 * HALF * COLS, transcendentals=0),
        name="merge_other",
    )(gradient, feedback, right_t)


def merge_own(gradient, feedback, right_t):
    return pl.pallas_call(
        merge_kernel,
        in_specs=[whole()] * 3,
        out_specs=[whole(), whole()],
        out_shape=[pltpu.VMEM((HALF, COLS), BF16), pltpu.VMEM((RANK, HALF), F32)],
        compiler_params=pltpu.CompilerParams(vmem_limit_bytes=16 * MIB),
        cost_estimate=pl.CostEstimate(flops=HALF * COLS * RANK * 2, bytes_accessed=4 * HALF * COLS, transcendentals=0),
        name="merge_own",
    )(gradient, feedback, right_t)


def right_kernel(merged_ref, left_ref, *refs):
    terms = jnp.concatenate(split(left_ref[...], 3), axis=0)
    total = jnp.dot(terms, merged_ref[...], preferred_element_type=F32)
    total = total[2 * RANK :] + total[RANK : 2 * RANK] + total[:RANK]
    for ref in refs[:-1]:
        total += ref[...]
    refs[-1][...] = total


def right_term(merged, left, *before):
    return pl.pallas_call(
        right_kernel,
        in_specs=[whole()] * (2 + len(before)),
        out_specs=whole(),
        out_shape=pltpu.VMEM((RANK, COLS), F32),
        compiler_params=pltpu.CompilerParams(vmem_limit_bytes=16 * MIB),
        cost_estimate=pl.CostEstimate(flops=4 * HALF * COLS * RANK, bytes_accessed=2 * HALF * COLS, transcendentals=0),
        name="right_other" if before else "right_own",
    )(merged, left, *before)


def basis_kernel(replicas, own_ref, other_ref, inverse_ref, basis_ref):
    own, other = own_ref[...], other_ref[...]
    gram = jnp.zeros((RANK, RANK), F32)
    for part in (own, other):
        gram += lax.dot_general(
            part, part, (((1,), (1,)), ((), ())), precision=lax.Precision.HIGHEST, preferred_element_type=F32
        )
    row = lax.broadcasted_iota(jnp.int32, (RANK, RANK), 0)
    column = lax.broadcasted_iota(jnp.int32, (RANK, RANK), 1)
    eye = jnp.where(row == column, 1.0, 0.0)
    inverse = eye
    for k in range(RANK):
        factor = jnp.where(row[:, :1] > k, gram[:, k : k + 1] / gram[k : k + 1, k : k + 1], 0.0)
        inverse -= factor * inverse[k : k + 1, :]
        gram -= factor * gram[k : k + 1, :]
    pivots = jnp.sum(gram * eye, axis=1, keepdims=True)
    inverse = inverse / jnp.sqrt(pivots)
    for k in range(RANK):
        column = inverse[:, k : k + 1] * (1.0 / replicas)
        inverse_ref[k * RANK : (k + 1) * RANK, :] = jnp.broadcast_to(column, (RANK, LANES))
    for part, start in ((own, 0), (other, HALF)):
        basis = jnp.zeros((RANK, HALF), F32)
        for k in range(RANK):
            basis += inverse[:, k : k + 1] * part[k : k + 1, :]
        high, low = split(basis, 2)
        packed = jnp.concatenate([high, high, low, low], axis=0)
        basis_ref[start : start + HALF, :] = packed.T


def make_basis(replicas, own, other):
    def body(*refs):
        basis_kernel(replicas, *refs)

    return pl.pallas_call(
        body,
        in_specs=[whole(), whole()],
        out_specs=[whole(), whole()],
        out_shape=[pltpu.VMEM((RANK * RANK, LANES), F32), pltpu.VMEM((ROWS, 4 * RANK), BF16)],
        compiler_params=pltpu.CompilerParams(vmem_limit_bytes=16 * MIB),
        cost_estimate=pl.CostEstimate(flops=4 * ROWS * RANK * RANK, bytes_accessed=4 * MIB, transcendentals=0),
        name="basis",
    )(own, other)


def final_kernel(
    own_ref, other_ref, basis_ref, inverse_ref, sum_ref, near_ref, wrap_ref, far_ref, mom_ref,
    fb_ref, mom_out_ref, right_ref,
    fb_buf, mom_buf, right_buf, fb_sem, mom_sem, right_sem,
):
    total = (sum_ref[...] + near_ref[...]) + (wrap_ref[...] + far_ref[...])
    pieces = []
    for start in range(0, COLS, LANES):
        piece = jnp.zeros((RANK, LANES), F32)
        for k in range(RANK):
            piece += inverse_ref[k * RANK : (k + 1) * RANK, :] * total[k : k + 1, start : start + LANES]
        pieces.append(piece)
    right = jnp.concatenate(pieces, axis=1)
    right_buf[...] = right
    copies = [pltpu.make_async_copy(right_buf, right_ref, right_sem.at[0])]
    copies[0].start()
    high, low = split(right, 2)
    pack = jnp.concatenate([high, low, high, low], axis=0)
    mine = own_half()
    for i, (start, count) in enumerate(WRITES):
        rows = pl.ds(start, count)
        merged_ref, half, low_row = (own_ref, mine, start) if start < HALF else (other_ref, 1 - mine, start - HALF)
        merged = merged_ref[pl.ds(low_row, count), :]
        approx = jnp.dot(basis_ref[rows, :], pack, preferred_element_type=F32)
        fb_buf[rows, :] = (merged.astype(F32) - approx).astype(BF16)
        target = fb_ref.at[0, pl.ds(pl.multiple_of(half * HALF + low_row, WRITES[0][1]), count), :]
        copies.append(pltpu.make_async_copy(fb_buf.at[rows, :], target, fb_sem.at[i]))
        copies[-1].start()
        if i == 0:
            count = mom_ref.shape[0]
            replica, per_half = lax.axis_index("replica"), HALF // count
            start = jnp.where(replica // per_half == mine, 0, HALF) + lax.rem(replica, per_half) * count
            mom_rows = pl.ds(pl.multiple_of(start, count), count)
            approx = jnp.dot(basis_ref[mom_rows, :], pack, preferred_element_type=F32)
            mom_buf[...] = (0.9 * mom_ref[...].astype(F32) + approx).astype(BF16)
            copies.append(pltpu.make_async_copy(mom_buf, mom_out_ref, mom_sem.at[0]))
            copies[-1].start()
    for copy in copies:
        copy.wait()


def finish(merged_own, merged_other, basis, inverse, parts, momentum):
    mom_rows = momentum.shape[0]
    return pl.pallas_call(
        final_kernel,
        in_specs=[whole()] * 9,
        out_specs=in_hbm(3),
        out_shape=[
            jax.ShapeDtypeStruct((1, ROWS, COLS), BF16),
            jax.ShapeDtypeStruct((mom_rows, COLS), BF16),
            jax.ShapeDtypeStruct((RANK, COLS), F32),
        ],
        scratch_shapes=[
            pltpu.VMEM((ROWS, COLS), BF16),
            pltpu.VMEM((mom_rows, COLS), BF16),
            pltpu.VMEM((RANK, COLS), F32),
            pltpu.SemaphoreType.DMA((len(WRITES),)),
            pltpu.SemaphoreType.DMA((1,)),
            pltpu.SemaphoreType.DMA((1,)),
        ],
        compiler_params=pltpu.CompilerParams(vmem_limit_bytes=20 * MIB),
        cost_estimate=pl.CostEstimate(flops=2 * ROWS * COLS * 32, bytes_accessed=4 * ROWS * COLS, transcendentals=0),
        name="finish",
    )(merged_own, merged_other, basis, inverse, *parts, momentum)


CORE, LOW = 16, {"y": 32, "z": 4, "x": 1}


def swap(x, masks):
    pairs = [(i, i ^ masks[i.bit_count() % 2]) for i in range(128)]
    return lax.ppermute(x, ("replica", "tensor"), pairs)


def ring_sum(x, axes):
    near = swap(x, [LOW[a] | CORE for a in axes])
    wrap = swap(x, [3 * LOW[a] for a in axes])
    return x + near + wrap + swap(x, [2 * LOW[a] | CORE for a in axes])


def sibling(x):
    return swap(x, [CORE] * 2)


def shards(gradient, feedback, momentum, right_init):
    gradient = pltpu.with_memory_space_constraint(gradient, pltpu.HBM)
    feedback = pltpu.with_memory_space_constraint(feedback, pltpu.HBM)
    right_t = pltpu.with_memory_space_constraint(right_init.T, pltpu.HBM)
    momentum = pltpu.with_memory_space_constraint(momentum, pltpu.VMEM)
    merged_other, send, *loaded = merge_other(gradient, feedback, right_t)
    received = sibling(send)
    merged_own, keep = merge_own(*loaded)
    own = keep + received
    for axes in ("yx", "xz", "zy"):
        own = ring_sum(own, axes)
    other = sibling(own)
    term = right_term(merged_other, other, right_term(merged_own, own))
    inverse, basis = make_basis(lax.axis_size("replica"), own, other)
    term = term + sibling(term)
    parts = [term, *(swap(term, [steps * LOW["y"] | CORE] * 2) for steps in (1, 3, 2))]
    feedback_out, momentum_out, right_t = finish(merged_own, merged_other, basis, inverse, parts, momentum)
    return feedback_out, momentum_out, right_t.T


def solution(mesh):
    placed = (
        P("replica", None, "tensor"),
        P("replica", None, "tensor"),
        P("replica", "tensor"),
        P("tensor", None),
    )
    return jax.shard_map(
        shards,
        mesh=mesh,
        in_specs=placed,
        out_specs=(P("replica", None, "tensor"), P("replica", "tensor"), P("tensor", None)),
        check_vma=False,
    )
```
